256 devices in a mesh: seq: 32 (over z_hi, y, x), chan: 8 (over z_lo, core).
Axes of the slice: x: 4, y: 4, z: 8 (z_hi: 2, z_lo: 4; z = z_hi * 4 + z_lo), core: 2. Of those that a mesh axis runs over, the one named last changes fastest.
Arguments:
- query_branch: bfloat16 [4096, 8192], P('seq', 'chan'), may hold values from -6 to 6
- key_branch: bfloat16 [4096, 8192], P('seq', 'chan'), may hold values from -6 to 6
- value_branch: bfloat16 [4096, 8192], P('seq', 'chan'), may hold values from -6 to 6
- short_filter: float32 [3, 3, 8192], P(None, None, 'chan'), may hold values from -1 to 1
- long_filter: float32 [8192, 4096], P(('chan', 'seq')), may hold values from -1.1 to 1.1
- out_weight: bfloat16 [8192, 8192], P('chan', 'seq'), may hold values from -0.0625 to 0.0625
- cotangent: bfloat16 [4096, 8192], P('seq', 'chan'), may hold values from -6 to 6
Outputs:
- block_output: bfloat16 [4096, 8192], P('seq', 'chan')
- query_grad: bfloat16 [4096, 8192], P('seq', 'chan')
- key_grad: bfloat16 [4096, 8192], P('seq', 'chan')
- value_grad: bfloat16 [4096, 8192], P('seq', 'chan')
- filter_grad: float32 [8192, 4096], P(('chan', 'seq'))
The draws below stay inside these ranges and needn't reach their ends.
All inputs are finite; a program needn't handle non-finite values.
Results may differ from the reference program's by a relative error of at most 0.017.
Values may be sent and summed in bfloat16 or wider, within the bound.
No kernel may reach another device: no remote copies, remote signals or barrier semaphores. Data moves between devices by JAX's collectives and lax.ppermute only.
A program may use at most 128 MiB of HBM per device.

```python
import jax
import jax.numpy as jnp
from jax import lax

D = 8192
TOKENS = 4096
N_CHAN = 8


def draw_long_filter(key, part):
    key = jax.random.fold_in(key, 11)
    noise_key, pick_key, slow_key, fast_key = jax.random.split(key, 4)
    fast_share = 0.5
    noise = jnp.clip(jax.random.normal(noise_key, (D, TOKENS), jnp.float32), -4.0, 4.0)
    fast = jax.random.bernoulli(pick_key, fast_share, (D, 1))
    slow_rate = jnp.exp(jax.random.uniform(slow_key, (D, 1), jnp.float32, jnp.log(0.1 / TOKENS), jnp.log(2.0 / TOKENS)))
    fast_rate = jnp.exp(jax.random.uniform(fast_key, (D, 1), jnp.float32, jnp.log(1.0 / 50.0), jnp.log(1.0 / 30.0)))
    rate = jnp.where(fast, fast_rate, slow_rate)
    lags = jnp.arange(TOKENS, dtype=jnp.float32)[None, :]
    amplitude = jnp.sqrt(2.0 * rate / (1.0 - jnp.exp(-2.0 * rate * TOKENS)))
    return amplitude * jnp.exp(-rate * lags) * noise


def levels(stream_key, dims, shards, least, largest):
    loudness, own = 1.0, jax.random.fold_in(stream_key, 6)
    for position, parts in shards:
        steps = jnp.exp(jax.random.uniform(jax.random.fold_in(own, position), (parts,), jnp.float32, least / len(shards), largest / len(shards)))
        loudness = loudness * jnp.repeat(steps, dims[position] // parts).reshape([-1 if axis == position else 1 for axis in range(len(dims))])
    return loudness


def centred(stream_key, dims, scale, reach, shards=(), held_as=jnp.bfloat16):
    values = scale * jax.random.normal(stream_key, dims, jnp.float32)
    if shards:
        values = values * levels(stream_key, dims, shards, -0.22, 0.18)
    return jnp.clip(values, -reach, reach).astype(held_as)


def setup_inputs(seed: int = 0) -> dict:
    keys = jax.random.split(jax.random.key(seed), 8)
    return {
        "query_branch": centred(keys[0], (TOKENS, D), 1.0, 6.0, ((0, 32), (1, 8))),
        "key_branch": centred(keys[1], (TOKENS, D), 1.0, 6.0, ((0, 32), (1, 8))),
        "value_branch": centred(keys[2], (TOKENS, D), 1.0, 6.0, ((0, 32), (1, 8))),
        "short_filter": jnp.clip(jax.random.uniform(keys[3], (3, 3, D), jnp.float32, -1.0, 1.0) * levels(keys[3], (3, 3, D), ((2, 8),), -0.4, 0.0), -1.0, 1.0),
        "long_filter": draw_long_filter(jax.random.fold_in(keys[7], 71), 0),
        "out_weight": centred(keys[5], (D, D), D ** -0.5, 0.0625, ((0, 8), (1, 32))),
        "cotangent": centred(keys[6], (TOKENS, D), 1.0, 6.0, ((0, 32), (1, 8))),
    }


def rounded(value):
    return lax.optimization_barrier(value.astype(jnp.bfloat16)).astype(jnp.float32)


def short_causal(signal, weights):
    extent = signal.shape[0]
    joined = jnp.concatenate([jnp.zeros_like(signal[:2]), signal], axis=0)
    return weights[0] * signal + weights[1] * joined[1:extent + 1] + weights[2] * joined[:extent]


def short_adjoint(signal, weights):
    extent = signal.shape[0]
    joined = jnp.concatenate([signal, jnp.zeros_like(signal[:2])], axis=0)
    return weights[0] * signal + weights[1] * joined[1:extent + 1] + weights[2] * joined[2:extent + 2]


def spectral(first, second, conjugate):
    extent = first.shape[1]
    first_spec = jnp.fft.rfft(first, n=2 * extent, axis=1)
    second_spec = jnp.fft.rfft(second, n=2 * extent, axis=1)
    if conjugate:
        second_spec = jnp.conj(second_spec)
    return jnp.fft.irfft(first_spec * second_spec, n=2 * extent, axis=1)[:, :extent]


def blockwise(first, second, conjugate):
    channels, extent = first.shape
    group = min(channels, 256)
    first_blocks = first.reshape(channels // group, group, extent)
    second_blocks = second.reshape(channels // group, group, extent)
    result = lax.map(lambda pair: spectral(pair[0], pair[1], conjugate), (first_blocks, second_blocks))
    return result.reshape(channels, extent)


def reference(query_branch, key_branch, value_branch, short_filter, long_filter, out_weight, cotangent):
    query_conv = short_causal(query_branch.astype(jnp.float32), short_filter[:, 0])
    key_conv = short_causal(key_branch.astype(jnp.float32), short_filter[:, 1])
    value_conv = short_causal(value_branch.astype(jnp.float32), short_filter[:, 2])
    gated = (key_conv * value_conv).astype(jnp.bfloat16)
    gated_rows = gated.astype(jnp.float32).T
    mixed = blockwise(gated_rows, long_filter, False).T.astype(jnp.bfloat16)
    mixed_value = mixed.astype(jnp.float32)
    product = (query_conv * mixed_value).astype(jnp.bfloat16)
    group = D // N_CHAN
    total = jnp.zeros((TOKENS, D), jnp.float32)
    for block_index in range(N_CHAN):
        lower = block_index * group
        partial_term = jnp.dot(product[:, lower:lower + group], out_weight[lower:lower + group], preferred_element_type=jnp.float32)
        total = total + rounded(partial_term)
    block_output = total.astype(jnp.bfloat16)
    out_grad = jnp.dot(cotangent, out_weight.T, preferred_element_type=jnp.float32)
    mixed_grad = (out_grad * query_conv).astype(jnp.bfloat16)
    mixed_rows = mixed_grad.astype(jnp.float32).T
    gated_grad = blockwise(mixed_rows, long_filter, True).T.astype(jnp.bfloat16)
    filter_grad = blockwise(mixed_rows, gated_rows, True) * (TOKENS ** -0.5)
    gated_value = gated_grad.astype(jnp.float32)
    query_grad = short_adjoint(out_grad * mixed_value, short_filter[:, 0]).astype(jnp.bfloat16)
    key_grad = short_adjoint(gated_value * value_conv, short_filter[:, 1]).astype(jnp.bfloat16)
    value_grad = short_adjoint(gated_value * key_conv, short_filter[:, 2]).astype(jnp.bfloat16)
    return (block_output, query_grad, key_grad, value_grad, filter_grad)
```

```python
import math

import jax
import jax.numpy as jnp
import numpy as np
from jax import lax
from jax.experimental import pallas as pl
from jax.experimental.pallas import tpu as pltpu
from jax.sharding import Mesh
from jax.sharding import PartitionSpec as P

SEQ = ("zh", "y", "x")
CHAN = ("zl", "core")
BF = jnp.bfloat16
F32 = jnp.float32
FAST = 128
GROUP = 8
VMEM = 40 * 1024 * 1024


def halves(value):
    high = np.asarray(value, np.float64).astype(jnp.bfloat16)
    low = (np.asarray(value, np.float64) - high.astype(np.float64)).astype(jnp.bfloat16)
    return high, low


def tables(length):
    rows = length // FAST
    slow = np.arange(rows)
    fast = np.arange(FAST)
    angle = 2 * math.pi * np.outer(slow + 0.25, slow) / rows
    first = np.concatenate([np.cos(angle), -np.sin(angle)], axis=0)
    high, low = halves(first)
    first_in = np.concatenate([high, low, high], axis=1)
    back = np.concatenate([np.cos(angle.T), -np.sin(angle.T)], axis=1) / length
    high, low = halves(back)
    first_out = np.concatenate([high, low, high], axis=1)
    twist = 2 * math.pi * np.outer(slow + 0.25, fast) / length
    twist = np.stack([np.cos(twist), np.sin(twist)]).astype(np.float32)
    turn = 2 * math.pi * np.outer(fast, fast) / FAST
    cos, sin = np.cos(turn), np.sin(turn)
    second_in = np.stack(halves(np.block([[cos, -sin], [sin, cos]])))
    second_out = np.stack(halves(np.block([[cos, sin], [-sin, cos]])))
    return first_in, first_out, twist, second_in, second_out


def split(value):
    high = value.astype(BF)
    return high, (value - high.astype(F32)).astype(BF)


def dot(first, second):
    return jnp.dot(first, second, preferred_element_type=F32)


def dot_wide(value, table):
    high, low = split(value)
    return dot(high, table[0]) + (dot(low, table[0]) + dot(high, table[1]))


def group_forward(held, group, first_in, twist, second_in):
    rows = twist.shape[1]
    channels = held.shape[0] // rows
    signal = jnp.concatenate(
        [held[pl.ds(group * GROUP + i, rows, stride=channels), :] for i in range(GROUP)], axis=1
    )
    high, low = split(signal)
    first = dot(first_in[...], jnp.concatenate([high, high, low], axis=0))
    cos, sin = twist[0], twist[1]
    parts = []
    for i in range(GROUP):
        real = first[:rows, i * FAST : (i + 1) * FAST]
        imag = first[rows:, i * FAST : (i + 1) * FAST]
        parts.append(jnp.concatenate([real * cos + imag * sin, imag * cos - real * sin], axis=1))
    return dot_wide(jnp.concatenate(parts, axis=0), second_in)


def group_inverse(spectrum, group, first_out, twist, second_out, held):
    rows = twist.shape[1]
    channels = held.shape[0] // rows
    back = dot_wide(spectrum, second_out)
    cos, sin = twist[0], twist[1]
    real_parts, imag_parts = [], []
    for i in range(GROUP):
        real = back[i * rows : (i + 1) * rows, :FAST]
        imag = back[i * rows : (i + 1) * rows, FAST:]
        real_parts.append(real * cos - imag * sin)
        imag_parts.append(real * sin + imag * cos)
    turned = jnp.concatenate(
        [jnp.concatenate(real_parts, axis=1), jnp.concatenate(imag_parts, axis=1)], axis=0
    )
    high, low = split(turned)
    result = dot(first_out[...], jnp.concatenate([high, high, low], axis=0))
    for i in range(GROUP):
        held[pl.ds(group * GROUP + i, rows, stride=channels), :] = result[:, i * FAST : (i + 1) * FAST]


def product_of(first, second, conjugate):
    first_re, first_im = first[:, :FAST], first[:, FAST:]
    second_re, second_im = second[:, :FAST], second[:, FAST:]
    if conjugate:
        return jnp.concatenate(
            [
                first_re * second_re + first_im * second_im,
                first_im * second_re - first_re * second_im,
            ],
            axis=1,
        )
    return jnp.concatenate(
        [
            first_re * second_re - first_im * second_im,
            first_re * second_im + first_im * second_re,
        ],
        axis=1,
    )


def filter_kernel(signal, first_in, twist, second_in, spectrum, held):
    rows = twist.shape[1]
    channels = signal.shape[0]
    for n1 in range(rows):
        held[n1 * channels : (n1 + 1) * channels, :] = signal[:, n1 * FAST : (n1 + 1) * FAST]
    step = GROUP * rows
    for group in range(channels // GROUP):
        spectrum[group * step : (group + 1) * step, :] = group_forward(
            held, group, first_in, twist, second_in
        )


def convolve_kernel(
    conjugate, signal, filter_spec, first_in, first_out, twist, second_in, second_out,
    result, spectrum, held, out,
):
    rows = twist.shape[1]
    channels = signal.shape[0] // rows
    held[...] = signal[...].astype(F32)
    step = GROUP * rows
    for group in range(channels // GROUP):
        here = slice(group * step, (group + 1) * step)
        spec = group_forward(held, group, first_in, twist, second_in)
        spectrum[here, :] = spec
        both = product_of(spec, filter_spec[here, :], conjugate)
        group_inverse(both, group, first_out, twist, second_out, out)
    result[...] = out[...].astype(result.dtype)


def filter_grad_kernel(first_spec, second_spec, first_out, twist, second_out, result, out):
    rows = twist.shape[1]
    channels = result.shape[0]
    scale = result.shape[1] ** -0.5
    step = GROUP * rows
    for group in range(channels // GROUP):
        here = slice(group * step, (group + 1) * step)
        both = product_of(first_spec[here, :], second_spec[here, :], True) * scale
        group_inverse(both, group, first_out, twist, second_out, out)
    for n1 in range(rows):
        result[:, n1 * FAST : (n1 + 1) * FAST] = out[n1 * channels : (n1 + 1) * channels, :]


def call(kernel, out_shape, scratch, *args):
    flops = 2 * 3 * 2 * 1024 * 256 * 256
    return pl.pallas_call(
        kernel,
        out_shape=out_shape,
        in_specs=[pl.BlockSpec(memory_space=pltpu.VMEM)] * len(args),
        out_specs=jax.tree.map(lambda _: pl.BlockSpec(memory_space=pltpu.VMEM), out_shape),
        scratch_shapes=scratch,
        compiler_params=pltpu.CompilerParams(vmem_limit_bytes=VMEM),
        cost_estimate=pl.CostEstimate(flops=flops, bytes_accessed=4 << 20, transcendentals=0),
    )(*args)


def causal(signal, before, weights):
    extent = signal.shape[0]
    joined = jnp.concatenate([before, signal], axis=0).astype(F32)
    return weights[0] * joined[2:] + weights[1] * joined[1 : extent + 1] + weights[2] * joined[:extent]


def adjoint(signal, after, weights):
    extent = signal.shape[0]
    joined = jnp.concatenate([signal, after], axis=0)
    return (
        weights[0] * joined[:extent] + weights[1] * joined[1 : extent + 1] + weights[2] * joined[2:]
    )


def swap(value, axis):
    return lax.ppermute(value, axis, [(0, 1), (1, 0)])


def to_channels(value):
    return lax.all_to_all(value.T, SEQ, split_axis=0, concat_axis=0, tiled=True)


def to_tokens(value):
    return lax.all_to_all(value, SEQ, split_axis=0, concat_axis=0, tiled=True).T


def shards(query, key, value, short_filter, long_filter, out_weight, cotangent):
    tokens, width = query.shape
    seq_count = lax.axis_size(SEQ)
    length = tokens * seq_count
    channels = width // seq_count
    zh, zl, core = lax.axis_index("zh"), lax.axis_index("zl"), lax.axis_index("core")
    upper, lower = zl // 2, zl % 2
    first_in, first_out, twist, second_in, second_out = (jnp.asarray(t) for t in tables(length))
    spec_type = jax.ShapeDtypeStruct((channels * length // FAST, 2 * FAST), F32)
    rows_type = jax.ShapeDtypeStruct((length // FAST * channels, FAST), BF)
    held = pltpu.VMEM(rows_type.shape, F32)

    weight = lax.all_gather(out_weight, ("y", "x"), axis=1, tiled=True)

    rows = jnp.concatenate([query[-2:], key[-2:], value[-2:]], axis=0)
    rows = lax.ppermute(rows, SEQ, [(i, i + 1) for i in range(seq_count - 1)])
    query_conv = causal(query, rows[0:2], short_filter[:, 0])
    key_conv = causal(key, rows[2:4], short_filter[:, 1])
    value_conv = causal(value, rows[4:6], short_filter[:, 2])
    gated = (key_conv * value_conv).astype(BF)
    gated_rows = to_channels(gated)

    filter_spec = call(filter_kernel, spec_type, [held], long_filter, first_in, twist, second_in)

    def links(k1, k2, back):
        pairs = []
        for a in range(2):
            for u in range(2):
                for v in range(2):
                    chip, owner = a * 4 + u * 2 + v, (u ^ k2) * 4 + a * 2 + (v ^ k1)
                    pairs.append((chip, owner) if back else (owner, chip))
        return pairs

    got = [[lax.ppermute(cotangent, ("zh", "zl"), links(k1, k2, False)) for k1 in range(2)] for k2 in range(2)]
    other_row = upper != zh
    mine = [jnp.where(other_row, got[1][k1], got[0][k1]) for k1 in range(2)]
    theirs = [jnp.where(other_row, got[0][k1], got[1][k1]) for k1 in range(2)]
    swapped = lower == 1
    ordered = jnp.stack(
        [
            jnp.stack([jnp.where(swapped, r[1], r[0]), jnp.where(swapped, r[0], r[1])], axis=1)
            for r in (mine, theirs)
        ]
    )
    beside = swap(ordered, "core")
    first_core = core == 0
    whole = jnp.stack(
        [jnp.where(first_core, ordered, beside), jnp.where(first_core, beside, ordered)], axis=3
    ).reshape(2 * tokens, 4 * width)

    mixed_rows, gated_spec = call(
        lambda *refs: convolve_kernel(False, *refs), (rows_type, spec_type), [held, held],
        gated_rows, filter_spec, first_in, first_out, twist, second_in, second_out,
    )
    mixed = to_tokens(mixed_rows).astype(F32)
    product = (query_conv * mixed).astype(BF)

    both = jnp.concatenate([product, swap(product, "zh")], axis=0)
    partial = jnp.dot(both, weight, preferred_element_type=F32).astype(BF)
    partial = partial.reshape(2, tokens, 2, 2, width)
    keep = lax.dynamic_index_in_dim(partial, core, 3, keepdims=False)
    give = lax.dynamic_index_in_dim(partial, 1 - core, 3, keepdims=False)
    chip = (keep.astype(F32) + swap(give, "core").astype(F32)).astype(BF)
    total = jnp.zeros((tokens, width), F32)
    for k2 in range(2):
        row = lax.dynamic_index_in_dim(chip, (upper ^ k2) ^ zh, 0, keepdims=False)
        for k1 in range(2):
            block = lax.dynamic_index_in_dim(row, lower ^ k1, 1, keepdims=False)
            total = total + lax.ppermute(block, ("zh", "zl"), links(k1, k2, True)).astype(F32)
    block_output = total.astype(BF)

    grads = lax.dot_general(whole, weight, (((1,), (1,)), ((), ())), preferred_element_type=F32)
    out_grad = grads[:tokens] + swap(grads[tokens:].astype(BF), "zh").astype(F32)
    mixed_grad = (out_grad * query_conv).astype(BF)
    mixed_grad_rows = to_channels(mixed_grad)
    gated_grad_rows, mixed_spec = call(
        lambda *refs: convolve_kernel(True, *refs), (rows_type, spec_type), [held, held],
        mixed_grad_rows, filter_spec, first_in, first_out, twist, second_in, second_out,
    )
    gated_grad = to_tokens(gated_grad_rows).astype(F32)
    filter_grad = call(
        filter_grad_kernel, jax.ShapeDtypeStruct((channels, length), F32), [held],
        mixed_spec, gated_spec, first_out, twist, second_out,
    )
    back = [(i + 1, i) for i in range(seq_count - 1)]
    query_conv_grad = out_grad * mixed
    query_after = lax.ppermute(query_conv_grad[:2], SEQ, back)
    query_grad = adjoint(query_conv_grad, query_after, short_filter[:, 0]).astype(BF)
    key_conv_grad = gated_grad * value_conv
    value_conv_grad = gated_grad * key_conv
    after = lax.ppermute(jnp.concatenate([key_conv_grad[:2], value_conv_grad[:2]], axis=0), SEQ, back)
    key_grad = adjoint(key_conv_grad, after[:2], short_filter[:, 1]).astype(BF)
    value_grad = adjoint(value_conv_grad, after[2:], short_filter[:, 2]).astype(BF)
    return (block_output, query_grad, key_grad, value_grad, filter_grad)


def solution(mesh):
    fine = Mesh(mesh.devices.reshape(2, 4, 4, 4, 2), SEQ + CHAN)
    return jax.shard_map(
        shards,
        mesh=fine,
        in_specs=(
            P(SEQ, CHAN),
            P(SEQ, CHAN),
            P(SEQ, CHAN),
            P(None, None, CHAN),
            P(CHAN + SEQ, None),
            P(CHAN, SEQ),
            P(SEQ, CHAN),
        ),
        out_specs=(
            P(SEQ, CHAN),
            P(SEQ, CHAN),
            P(SEQ, CHAN),
            P(SEQ, CHAN),
            P(CHAN + SEQ, None),
        ),
        check_vma=False,
    )
```

```python
import functools
import math

import jax
import jax.numpy as jnp
import numpy as np
from jax import lax
from jax.experimental import pallas as pl
from jax.experimental.pallas import tpu as pltpu
from jax.sharding import Mesh
from jax.sharding import PartitionSpec as P

SEQ = ("zh", "y", "x")
CHAN = ("zl", "core")
BF = jnp.bfloat16
F32 = jnp.float32
FAST = 128
GROUP = 8
VMEM = 60 * 1024 * 1024


def halves(value):
    high = np.asarray(value, np.float64).astype(jnp.bfloat16)
    low = (np.asarray(value, np.float64) - high.astype(np.float64)).astype(jnp.bfloat16)
    return high, low


def tables(length):
    rows = length // FAST
    slow = np.arange(rows)
    fast = np.arange(FAST)
    angle = 2 * math.pi * np.outer(slow + 0.25, slow) / rows
    first = np.concatenate([np.cos(angle), -np.sin(angle)], axis=0)
    high, low = halves(first)
    first_in = np.concatenate([high, low, high], axis=1)
    back = np.concatenate([np.cos(angle.T), -np.sin(angle.T)], axis=1) / length
    high, low = halves(back)
    first_out = np.concatenate([high, low, high], axis=1)
    twist = 2 * math.pi * np.outer(slow + 0.25, fast) / length
    twist = np.stack([np.cos(twist), np.sin(twist)]).astype(np.float32)
    turn = 2 * math.pi * np.outer(fast, fast) / FAST
    cos, sin = np.cos(turn), np.sin(turn)
    second_in = np.stack(halves(np.block([[cos, -sin], [sin, cos]])))
    second_out = np.stack(halves(np.block([[cos, sin], [-sin, cos]])))
    return first_in, first_out, twist, second_in, second_out


def split(value):
    high = value.astype(BF)
    return high, (value - high.astype(F32)).astype(BF)


def dot(first, second):
    return jnp.dot(first, second, preferred_element_type=F32)


def dot_wide(value, table):
    high, low = split(value)
    return dot(high, table[0]) + (dot(low, table[0]) + dot(high, table[1]))


def group_forward(held, group, first_in, twist, second_in):
    rows = twist.shape[1]
    channels = held.shape[0] // rows
    signal = jnp.concatenate(
        [held[pl.ds(group * GROUP + i, rows, stride=channels), :] for i in range(GROUP)], axis=1
    )
    high, low = split(signal)
    first = dot(first_in[...], jnp.concatenate([high, high, low], axis=0))
    cos, sin = twist[0], twist[1]
    parts = []
    for i in range(GROUP):
        real = first[:rows, i * FAST : (i + 1) * FAST]
        imag = first[rows:, i * FAST : (i + 1) * FAST]
        parts.append(jnp.concatenate([real * cos + imag * sin, imag * cos - real * sin], axis=1))
    return dot_wide(jnp.concatenate(parts, axis=0), second_in)


def group_inverse(spectrum, group, first_out, twist, second_out, held):
    rows = twist.shape[1]
    channels = held.shape[0] // rows
    back = dot_wide(spectrum, second_out)
    cos, sin = twist[0], twist[1]
    real_parts, imag_parts = [], []
    for i in range(GROUP):
        real = back[i * rows : (i + 1) * rows, :FAST]
        imag = back[i * rows : (i + 1) * rows, FAST:]
        real_parts.append(real * cos - imag * sin)
        imag_parts.append(real * sin + imag * cos)
    turned = jnp.concatenate(
        [jnp.concatenate(real_parts, axis=1), jnp.concatenate(imag_parts, axis=1)], axis=0
    )
    high, low = split(turned)
    result = dot(first_out[...], jnp.concatenate([high, high, low], axis=0))
    for i in range(GROUP):
        held[pl.ds(group * GROUP + i, rows, stride=channels), :] = result[:, i * FAST : (i + 1) * FAST]


def product_of(first, second, conjugate):
    first_re, first_im = first[:, :FAST], first[:, FAST:]
    second_re, second_im = second[:, :FAST], second[:, FAST:]
    if conjugate:
        return jnp.concatenate(
            [
                first_re * second_re + first_im * second_im,
                first_im * second_re - first_re * second_im,
            ],
            axis=1,
        )
    return jnp.concatenate(
        [
            first_re * second_re - first_im * second_im,
            first_re * second_im + first_im * second_re,
        ],
        axis=1,
    )


def filter_kernel(signal, first_in, twist, second_in, spectrum, held):
    rows = twist.shape[1]
    channels = signal.shape[0]
    for n1 in range(rows):
        held[n1 * channels : (n1 + 1) * channels, :] = signal[:, n1 * FAST : (n1 + 1) * FAST]
    step = GROUP * rows
    for group in range(channels // GROUP):
        spectrum[group * step : (group + 1) * step, :] = group_forward(
            held, group, first_in, twist, second_in
        )


def convolve_kernel(
    conjugate, signal, filter_spec, first_in, first_out, twist, second_in, second_out,
    result, spectrum, held, out,
):
    rows = twist.shape[1]
    channels = held.shape[0] // rows
    step = GROUP * rows

    def line(n1):
        return slice(n1 * channels, (n1 + 1) * channels)

    if len(signal.shape) == 2:
        held[...] = signal[...].astype(F32)
    else:
        for n1 in range(rows):
            held[line(n1), :] = signal[n1 % signal.shape[0], n1 // signal.shape[0]].astype(F32)
    for group in range(channels // GROUP):
        here = slice(group * step, (group + 1) * step)
        spec = group_forward(held, group, first_in, twist, second_in)
        spectrum[here, :] = spec
        both = product_of(spec, filter_spec[here, :], conjugate)
        group_inverse(both, group, first_out, twist, second_out, out)
    if len(result.shape) == 2:
        result[...] = out[...].astype(result.dtype)
    else:
        for n1 in range(rows):
            result[n1 % result.shape[0], n1 // result.shape[0]] = out[line(n1), :].astype(result.dtype)


def filter_grad_kernel(first_spec, second_spec, first_out, twist, second_out, result, out):
    rows = twist.shape[1]
    channels = result.shape[0]
    scale = result.shape[1] ** -0.5
    step = GROUP * rows
    for group in range(channels // GROUP):
        here = slice(group * step, (group + 1) * step)
        both = product_of(first_spec[here, :], second_spec[here, :], True) * scale
        group_inverse(both, group, first_out, twist, second_out, out)
    for n1 in range(rows):
        result[:, n1 * FAST : (n1 + 1) * FAST] = out[n1 * channels : (n1 + 1) * channels, :]


def whole(array):
    return pl.BlockSpec(array.shape, lambda *_: (0,) * len(array.shape))


def call(kernel, out_shape, scratch, *args, grid=(), specs=None, out_specs=None, flops=1024):
    specs = specs or {}
    return pl.pallas_call(
        kernel,
        out_shape=out_shape,
        grid=grid,
        in_specs=[specs.get(i, whole(arg)) for i, arg in enumerate(args)],
        out_specs=out_specs or jax.tree.map(whole, out_shape),
        scratch_shapes=scratch,
        compiler_params=pltpu.CompilerParams(vmem_limit_bytes=VMEM),
        cost_estimate=pl.CostEstimate(flops=flops, bytes_accessed=1024, transcendentals=0),
    )(*args)


def position(*names):
    return tuple(lax.axis_index(name) for name in names)


def shape_of(dims, dtype):
    return jax.ShapeDtypeStruct(dims, dtype)


PAD = 16


def taps_of(short_filter, branch, columns=slice(None)):
    return [short_filter[tap, branch : branch + 1, columns] for tap in range(3)]


def causal_rows(joined, taps):
    extent = joined.shape[0] - 8
    return (
        taps[0] * joined[8:] + taps[1] * joined[7 : 7 + extent] + taps[2] * joined[6 : 6 + extent]
    )


def causal(signal, halo, short_filter, branch):
    before = halo[branch * PAD : (branch + 1) * PAD, :].astype(F32)[PAD - 8 :]
    joined = jnp.concatenate([before, signal[...].astype(F32)], axis=0)
    return causal_rows(joined, taps_of(short_filter, branch))


def adjoint(signal, after, taps):
    extent = signal.shape[0]
    joined = jnp.concatenate([signal, after], axis=0)
    return (
        taps[0] * joined[:extent]
        + taps[1] * joined[1 : extent + 1]
        + taps[2] * joined[2 : extent + 2]
    )


def turned(value):
    return jnp.concatenate(
        [value[:, i : i + 128].T for i in range(0, value.shape[1], 128)], axis=0
    )


def turned_back(rows):
    rows = rows.astype(F32)
    return jnp.concatenate(
        [rows[i : i + 128].T for i in range(0, rows.shape[0], 128)], axis=1
    )


def gated_kernel(key, value, halo, short_filter, result):
    gated = causal(key, halo, short_filter, 1) * causal(value, halo, short_filter, 2)
    result[...] = turned(gated).astype(BF)


def columns_of(which, width):
    return pl.ds(pl.multiple_of((lax.axis_index("zh") ^ which) * width, width), width)


def halo_kernel(query, key, value, result):
    for branch, ref in enumerate((query, key, value)):
        result[branch * PAD : (branch + 1) * PAD, :] = ref[...]


def query_split_kernel(query, halo, keep, give):
    for which, result in ((0, keep), (1, give)):
        columns = columns_of(which, result.shape[1])
        result[:PAD, :] = halo[:PAD, columns]
        result[PAD:, :] = query[:, columns]


def query_conv(query, short_filter):
    taps = taps_of(short_filter, 0, columns_of(0, query.shape[1]))
    return causal_rows(query[...].astype(F32)[PAD - 8 :], taps)


def product_kernel(own, other, short_filter, mixed_rows, product, mixed):
    for half, query in enumerate((own, other)):
        there = lax.axis_index("zh") ^ half
        sources, _, channels, _ = mixed_rows.shape
        blocks = []
        for first in range(0, sources * channels, 128):
            rows = [
                mixed_rows[s, there] for s in range(first // channels, (first + 128) // channels)
            ]
            blocks.append(jnp.concatenate(rows, axis=0).astype(F32).T)
        here = jnp.concatenate(blocks, axis=1)
        mixed[half] = here.astype(BF)
        product[half] = (query_conv(query, short_filter) * here).astype(BF)


def mixed_grad_kernel(
    keep, beside, own, other, short_filter, mixed, result, conv_grad, edge
):
    channels = result.shape[2]
    for half, query in enumerate((own, other)):
        out_grad = keep[half] + beside[1 - half].astype(F32)
        rows = turned(out_grad * query_conv(query, short_filter)).astype(BF)
        for s in range(result.shape[0]):
            result[s, lax.axis_index("zh") ^ half] = rows[s * channels : (s + 1) * channels]
        query_grad = out_grad * mixed[half].astype(F32)
        conv_grad[half] = query_grad
        edge[half] = query_grad[:8]


def query_grad_kernel(conv_grad, after, short_filter, keep, give):
    taps = taps_of(short_filter, 0, columns_of(0, keep.shape[1]))
    zh, y, x = position("zh", "y", "x")
    last = (y == 3) & (x == 3)
    for half, result in ((0, keep), (1, give)):
        beyond = jnp.where((zh ^ half) == 0, after[1 - half], 0.0)
        rows = jnp.where(last, beyond, after[half])
        result[...] = adjoint(conv_grad[half], rows, taps).astype(BF)


def query_join_kernel(keep, beside, result):
    width = keep.shape[1]
    result[:, columns_of(0, width)] = keep[...]
    result[:, columns_of(1, width)] = beside[...]


def edge_kernel(key, value, halo, short_filter, gated_grad_rows, key_grad, value_grad, edge):
    gated_grad = turned_back(gated_grad_rows[...])
    key_here = gated_grad * causal(value, halo, short_filter, 2)
    value_here = gated_grad * causal(key, halo, short_filter, 1)
    key_grad[...] = key_here
    value_grad[...] = value_here
    edge[:8] = key_here[:8]
    edge[8:] = value_here[:8]


def last_kernel(key_conv_grad, value_conv_grad, after, short_filter, key_grad, value_grad):
    key_grad[...] = adjoint(key_conv_grad[...], after[:8], taps_of(short_filter, 1)).astype(BF)
    value_grad[...] = adjoint(value_conv_grad[...], after[8:], taps_of(short_filter, 2)).astype(BF)


def backward_kernel(cot, beside, weight, keep, give, both, total):
    row = pl.program_id(0)
    zh, zl, core = position("zh", "zl", "core")
    tokens, half_width = keep.shape[1:]

    @pl.when(row == 0)
    def _():
        both[0] = cot[...]
        both[1] = beside[...]
        total[...] = jnp.zeros_like(total)

    which, k1 = (row % 2) ^ core, (row // 2) ^ (zl % 2)
    lines = jnp.concatenate(
        [both[which, (half ^ zh ^ (zl // 2)) * 2 + k1] for half in range(2)], axis=0
    )
    across = (((1,), (1,)), ((), ()))
    for part in range(2):
        here = slice(part * half_width, (part + 1) * half_width)
        rows = jnp.concatenate([weight[i, here, :] for i in range(4)], axis=1)
        total[part] += lax.dot_general(lines, rows, across, preferred_element_type=F32)

    @pl.when(row == 3)
    def _():
        for half in range(2):
            here = slice(half * tokens, (half + 1) * tokens)
            keep[half] = total[zh, here, :]
            give[half] = total[1 - zh, here, :].astype(BF)


def forward_kernel(product, beside, weight, result):
    zh = lax.axis_index("zh")
    tokens = product.shape[1]
    own = jnp.concatenate([product[0], product[1]], axis=0)
    other = jnp.concatenate([beside[1], beside[0]], axis=0)
    left = jnp.concatenate(
        [jnp.where(zh == 0, own, other), jnp.where(zh == 0, other, own)], axis=1
    )
    rows = jnp.concatenate([weight[i] for i in range(4)], axis=1)
    term = jnp.dot(left, rows, preferred_element_type=F32).astype(BF)
    for half in range(2):
        result[half ^ zh, 0] = term[half * tokens : (half + 1) * tokens]


def swap(value, axis):
    return lax.ppermute(value, axis, [(0, 1), (1, 0)])


def exchange(value):
    return lax.all_to_all(value, ("y", "x"), split_axis=0, concat_axis=0, tiled=True)


def once(value, *others):
    return lax.optimization_barrier((value,) + others)[0]


def shards(query, key, value, short_filter, long_filter, out_weight, cotangent):
    tokens, width = query.shape
    seq_count = lax.axis_size(SEQ)
    length = tokens * seq_count
    channels = width // seq_count
    first_in, first_out, twist, second_in, second_out = (jnp.asarray(t) for t in tables(length))
    spec_type = shape_of((channels * length // FAST, 2 * FAST), F32)
    rows_type = shape_of((length // FAST * channels, FAST), BF)
    tokens_bf, tokens_f32 = shape_of((tokens, width), BF), shape_of((tokens, width), F32)
    held = pltpu.VMEM(rows_type.shape, F32)

    half = width // 2
    split_type = shape_of((16, 2, channels, FAST), BF)
    halves_bf = shape_of((2, tokens, half), BF)
    halves_f32 = shape_of((2, tokens, half), F32)

    weight = lax.all_gather(out_weight, ("y", "x"))

    def links(k1, k2, back):
        result = []
        for a in range(2):
            for u in range(2):
                for v in range(2):
                    chip, owner = a * 4 + u * 2 + v, (u ^ k2) * 4 + a * 2 + (v ^ k1)
                    result.append((chip, owner) if back else (owner, chip))
        return result


    last_rows = pl.BlockSpec((PAD, width), lambda *_: (tokens // PAD - 1, 0))
    halo = call(
        halo_kernel, shape_of((3 * PAD, width), BF), [], query, key, value,
        grid=(1,), specs={i: last_rows for i in range(3)},
    )
    halo = lax.ppermute(halo, SEQ, [(i, i + 1) for i in range(seq_count - 1)])
    filter_spec = call(filter_kernel, spec_type, [held], long_filter, first_in, twist, second_in)
    halo = once(halo, filter_spec)
    gated_rows = call(gated_kernel, rows_type, [], key, value, halo, short_filter)
    gated_rows = lax.all_to_all(gated_rows, SEQ, split_axis=0, concat_axis=0, tiled=True)

    query_type = shape_of((PAD + tokens, half), BF)
    query_own, query_other = call(
        query_split_kernel, (query_type, query_type), [], query, halo
    )
    query_other = swap(query_other, "zh")

    cot_there = once(cotangent, gated_rows)
    blocks = [
        lax.ppermute(cot_there, ("zh", "zl"), links(k1, k2, False)) for k2 in range(2) for k1 in range(2)
    ]
    gated_rows = once(gated_rows, query_other)
    mixed_rows, gated_spec = call(
        functools.partial(convolve_kernel, False), (split_type, spec_type), [held, held],
        gated_rows, filter_spec, first_in, first_out, twist, second_in, second_out,
    )
    mixed_rows = exchange(mixed_rows)
    product, mixed = call(
        product_kernel, (halves_bf, halves_bf), [],
        query_own, query_other, short_filter, mixed_rows,
    )
    product_beside = swap(product, "zh")
    got = jnp.stack(once(tuple(blocks), product))
    got_beside = swap(got, "core")

    four = pl.BlockSpec((4,) + out_weight.shape, lambda row: (row, 0, 0))
    grads, grads_beside = call(
        backward_kernel, (halves_f32, halves_bf),
        [pltpu.VMEM((2, 4, tokens, width), BF), pltpu.VMEM((2, 2 * tokens, half), F32)],
        got, got_beside, weight, grid=(4,), specs={2: four},
    )
    product_beside = once(product_beside, grads_beside)
    grads_beside = swap(grads_beside, "zh")

    partial = call(
        forward_kernel, shape_of((2, 4, tokens, width), BF), [],
        product, product_beside, weight, grid=(4,), specs={2: four}, flops=1 << 34,
        out_specs=pl.BlockSpec((2, 1, tokens, width), lambda row: (0, row, 0, 0)),
    )
    summed = lax.psum_scatter(partial.reshape(8, tokens, width), CHAN, scatter_dimension=0)
    block_output = lax.ppermute(summed, ("zh", "zl"), links(0, 0, True))

    mixed_grad_rows, query_conv_grad, query_edge = call(
        mixed_grad_kernel, (split_type, halves_f32, shape_of((2, 8, half), F32)), [],
        grads, once(grads_beside, partial), query_own, query_other, short_filter, mixed, flops=1 << 33,
    )
    query_after = lax.ppermute(query_edge, ("y", "x"), [((i + 1) % 16, i) for i in range(16)])
    mixed_grad_rows = exchange(mixed_grad_rows)
    half_type = shape_of((tokens, half), BF)
    query_grad, query_grad_other = call(
        query_grad_kernel, (half_type, half_type), [],
        query_conv_grad, query_after, short_filter,
    )
    gated_grad_rows, mixed_spec = call(
        functools.partial(convolve_kernel, True), (rows_type, spec_type), [held, held],
        once(mixed_grad_rows, query_grad_other), filter_spec, first_in, first_out, twist, second_in, second_out,
        flops=1 << 35,
    )
    gated_grad_rows = lax.all_to_all(gated_grad_rows, SEQ, split_axis=0, concat_axis=0, tiled=True)
    filter_grad = call(
        filter_grad_kernel, shape_of((channels, length), F32), [held],
        mixed_spec, gated_spec, first_out, twist, second_out,
    )
    back = [(i + 1, i) for i in range(seq_count - 1)]
    query_grad_other = swap(query_grad_other, "zh")
    query_grad = call(
        query_join_kernel, tokens_bf, [], query_grad, query_grad_other
    )
    key_conv_grad, value_conv_grad, edge = call(
        edge_kernel, (tokens_f32, tokens_f32, shape_of((16, width), F32)), [],
        key, value, halo, short_filter, gated_grad_rows, flops=1 << 33,
    )
    after = lax.ppermute(edge, SEQ, back)
    key_grad, value_grad = call(
        last_kernel, (tokens_bf, tokens_bf), [], key_conv_grad, value_conv_grad, once(after, filter_grad), short_filter
    )
    return (block_output, query_grad, key_grad, value_grad, filter_grad)


def solution(mesh):
    fine = Mesh(mesh.devices.reshape(2, 4, 4, 4, 2), SEQ + CHAN)
    return jax.shard_map(
        shards,
        mesh=fine,
        in_specs=(
            P(SEQ, CHAN),
            P(SEQ, CHAN),
            P(SEQ, CHAN),
            P(None, None, CHAN),
            P(CHAN + SEQ, None),
            P(CHAN, SEQ),
            P(SEQ, CHAN),
        ),
        out_specs=(
            P(SEQ, CHAN),
            P(SEQ, CHAN),
            P(SEQ, CHAN),
            P(SEQ, CHAN),
            P(CHAN + SEQ, None),
        ),
        check_vma=False,
    )
```

```python
import functools
import math

import jax
import jax.numpy as jnp
import numpy as np
from jax import lax
from jax.experimental import pallas as pl
from jax.experimental.pallas import tpu as pltpu
from jax.sharding import Mesh
from jax.sharding import PartitionSpec as P

SEQ = ("zh", "y", "x")
CHAN = ("zl", "core")
BF = jnp.bfloat16
F32 = jnp.float32
FAST = 128
GROUP = 8
VMEM = 65408 * 1024


def halves(value):
    high = np.asarray(value, np.float64).astype(jnp.bfloat16)
    low = (np.asarray(value, np.float64) - high.astype(np.float64)).astype(jnp.bfloat16)
    return high, low


def tables(length):
    rows = length // FAST
    slow = np.arange(rows)
    fast = np.arange(FAST)
    angle = 2 * math.pi * np.outer(slow + 0.25, slow) / rows
    first = np.concatenate([np.cos(angle), -np.sin(angle)], axis=0)
    high, low = halves(first)
    first_in = np.concatenate([high, low, high], axis=1)
    back = np.concatenate([np.cos(angle.T), -np.sin(angle.T)], axis=1) / length
    high, low = halves(back)
    first_out = np.concatenate([high, low, high], axis=1)
    twist = 2 * math.pi * np.outer(slow + 0.25, fast) / length
    twist = np.stack([np.cos(twist), np.sin(twist)]).astype(np.float32)
    turn = 2 * math.pi * np.outer(fast, fast) / FAST
    cos, sin = np.cos(turn), np.sin(turn)
    second_in = np.stack(halves(np.block([[cos, -sin], [sin, cos]])))
    second_out = np.stack(halves(np.block([[cos, sin], [-sin, cos]])))
    return first_in, first_out, twist, second_in, second_out


def split(value):
    high = value.astype(BF)
    return high, (value - high.astype(F32)).astype(BF)


def dot(first, second):
    return jnp.dot(first, second, preferred_element_type=F32)


def dot_wide(value, table):
    high, low = split(value)
    return dot(high, table[0]) + (dot(low, table[0]) + dot(high, table[1]))


def group_forward(held, group, first_in, twist, second_in):
    rows = twist.shape[1]
    channels = held.shape[0] // rows
    signal = jnp.concatenate(
        [held[pl.ds(group * GROUP + i, rows, stride=channels), :] for i in range(GROUP)], axis=1
    )
    high, low = split(signal)
    first = dot(first_in[...], jnp.concatenate([high, high, low], axis=0))
    cos, sin = twist[0], twist[1]
    parts = []
    for i in range(GROUP):
        real = first[:rows, i * FAST : (i + 1) * FAST]
        imag = first[rows:, i * FAST : (i + 1) * FAST]
        parts.append(jnp.concatenate([real * cos + imag * sin, imag * cos - real * sin], axis=1))
    return dot_wide(jnp.concatenate(parts, axis=0), second_in)


def group_inverse(spectrum, group, first_out, twist, second_out, held):
    rows = twist.shape[1]
    channels = held.shape[0] // rows
    back = dot_wide(spectrum, second_out)
    cos, sin = twist[0], twist[1]
    real_parts, imag_parts = [], []
    for i in range(GROUP):
        real = back[i * rows : (i + 1) * rows, :FAST]
        imag = back[i * rows : (i + 1) * rows, FAST:]
        real_parts.append(real * cos - imag * sin)
        imag_parts.append(real * sin + imag * cos)
    turned = jnp.concatenate(
        [jnp.concatenate(real_parts, axis=1), jnp.concatenate(imag_parts, axis=1)], axis=0
    )
    high, low = split(turned)
    result = dot(first_out[...], jnp.concatenate([high, high, low], axis=0))
    for i in range(GROUP):
        held[pl.ds(group * GROUP + i, rows, stride=channels), :] = result[:, i * FAST : (i + 1) * FAST]


def product_of(first, second, conjugate):
    first_re, first_im = first[:, :FAST], first[:, FAST:]
    second_re, second_im = second[:, :FAST], second[:, FAST:]
    if conjugate:
        return jnp.concatenate(
            [
                first_re * second_re + first_im * second_im,
                first_im * second_re - first_re * second_im,
            ],
            axis=1,
        )
    return jnp.concatenate(
        [
            first_re * second_re - first_im * second_im,
            first_re * second_im + first_im * second_re,
        ],
        axis=1,
    )


def filter_kernel(signal, first_in, twist, second_in, spectrum, held):
    rows = twist.shape[1]
    channels = signal.shape[0]
    for n1 in range(rows):
        held[n1 * channels : (n1 + 1) * channels, :] = signal[:, n1 * FAST : (n1 + 1) * FAST]
    step = GROUP * rows
    for group in range(channels // GROUP):
        spectrum[group * step : (group + 1) * step, :] = group_forward(
            held, group, first_in, twist, second_in
        )


def convolve_kernel(
    conjugate, signal, filter_spec, first_in, first_out, twist, second_in, second_out,
    result, spectrum, held, out,
):
    rows = twist.shape[1]
    channels = held.shape[0] // rows
    step = GROUP * rows

    def line(n1):
        return slice(n1 * channels, (n1 + 1) * channels)

    if len(signal.shape) == 2:
        held[...] = signal[...].astype(F32)
    else:
        for n1 in range(rows):
            held[line(n1), :] = signal[n1 % signal.shape[0], n1 // signal.shape[0]].astype(F32)
    for group in range(channels // GROUP):
        here = slice(group * step, (group + 1) * step)
        spec = group_forward(held, group, first_in, twist, second_in)
        spectrum[here, :] = spec
        both = product_of(spec, filter_spec[here, :], conjugate)
        group_inverse(both, group, first_out, twist, second_out, out)
    if len(result.shape) == 4:
        for n1 in range(rows):
            result[n1 % result.shape[0], n1 // result.shape[0]] = out[line(n1), :].astype(result.dtype)
        return
    count = FAST // channels
    place = lax.axis_index("x")
    column = lax.broadcasted_iota(jnp.int32, (8, FAST), 1)
    mine = (column >= place * channels) & (column < (place + 1) * channels)
    empty = jnp.zeros((PAD - 8, FAST), F32)
    for n1 in range(rows):
        result[n1, :channels] = out[line(n1), :].astype(result.dtype)
        if n1 % count == 0:
            ahead = out[n1 * channels : (n1 + count) * channels, :].T[:8]
        if n1 > 0:
            moved = pltpu.roll(ahead, (place + 4 - n1 % count) % 4 * channels, 1)
            strip = jnp.concatenate([jnp.where(mine, moved, 0.0), empty], axis=0)
            result[n1 - 1, channels:] = strip.astype(result.dtype)
    result[rows - 1, channels:] = jnp.zeros((PAD, FAST), result.dtype)


def filter_grad_kernel(first_spec, second_spec, first_out, twist, second_out, result, out):
    rows = twist.shape[1]
    channels = result.shape[0]
    scale = result.shape[1] ** -0.5
    step = GROUP * rows
    for group in range(channels // GROUP):
        here = slice(group * step, (group + 1) * step)
        both = product_of(first_spec[here, :], second_spec[here, :], True) * scale
        group_inverse(both, group, first_out, twist, second_out, out)
    for n1 in range(rows):
        result[:, n1 * FAST : (n1 + 1) * FAST] = out[n1 * channels : (n1 + 1) * channels, :]


def whole(array):
    return pl.BlockSpec(array.shape, lambda *_: (0,) * len(array.shape))


def call(kernel, out_shape, scratch, *args, grid=(), specs=None, out_specs=None, flops=1024):
    specs = specs or {}
    return pl.pallas_call(
        kernel,
        out_shape=out_shape,
        grid=grid,
        in_specs=[specs.get(i, whole(arg)) for i, arg in enumerate(args)],
        out_specs=out_specs or jax.tree.map(whole, out_shape),
        scratch_shapes=scratch,
        compiler_params=pltpu.CompilerParams(vmem_limit_bytes=VMEM),
        cost_estimate=pl.CostEstimate(flops=flops, bytes_accessed=1024, transcendentals=0),
    )(*args)


def position(*names):
    return tuple(lax.axis_index(name) for name in names)


def shape_of(dims, dtype):
    return jax.ShapeDtypeStruct(dims, dtype)


PAD = 16


def taps_of(short_filter, branch, columns=slice(None)):
    return [short_filter[tap, branch : branch + 1, columns] for tap in range(3)]


def causal_rows(joined, taps):
    extent = joined.shape[0] - 8
    return (
        taps[0] * joined[8:] + taps[1] * joined[7 : 7 + extent] + taps[2] * joined[6 : 6 + extent]
    )


def causal(signal, halo, short_filter, branch):
    before = halo[branch * PAD : (branch + 1) * PAD, :].astype(F32)[PAD - 8 :]
    joined = jnp.concatenate([before, signal[...].astype(F32)], axis=0)
    return causal_rows(joined, taps_of(short_filter, branch))


def adjoint(signal, after, taps):
    extent = signal.shape[0]
    joined = jnp.concatenate([signal, after], axis=0)
    return (
        taps[0] * joined[:extent]
        + taps[1] * joined[1 : extent + 1]
        + taps[2] * joined[2 : extent + 2]
    )


def turned(value):
    return jnp.concatenate(
        [value[:, i : i + 128].T for i in range(0, value.shape[1], 128)], axis=0
    )


def turned_back(rows):
    rows = rows.astype(F32)
    return jnp.concatenate(
        [rows[i : i + 128].T for i in range(0, rows.shape[0], 128)], axis=1
    )


def gated_kernel(key, value, halo, short_filter, result):
    gated = causal(key, halo, short_filter, 1) * causal(value, halo, short_filter, 2)
    result[...] = turned(gated).astype(BF)


def columns_of(which, width):
    return pl.ds(pl.multiple_of((lax.axis_index("zh") ^ which) * width, width), width)


def halo_kernel(query, key, value, result):
    for branch, ref in enumerate((query, key, value)):
        result[branch * PAD : (branch + 1) * PAD, :] = ref[...]


def query_split_kernel(query, halo, keep, give):
    for which, result in ((0, keep), (1, give)):
        columns = columns_of(which, result.shape[1])
        result[:PAD, :] = halo[:PAD, columns]
        result[PAD:, :] = query[:, columns]


def query_conv(query, short_filter):
    taps = taps_of(short_filter, 0, columns_of(0, query.shape[1]))
    return causal_rows(query[...].astype(F32)[PAD - 8 :], taps)


def product_kernel(own, other, short_filter, mixed_rows, product, mixed):
    for half, query in enumerate((own, other)):
        there = lax.axis_index("zh") ^ half
        sources, _, channels, _ = mixed_rows.shape
        blocks = []
        for first in range(0, sources * channels, 128):
            rows = [
                mixed_rows[s, there] for s in range(first // channels, (first + 128) // channels)
            ]
            blocks.append(jnp.concatenate(rows, axis=0).astype(F32).T)
        here = jnp.concatenate(blocks, axis=1)
        mixed[half] = here.astype(BF)
        product[half] = (query_conv(query, short_filter) * here).astype(BF)


def mixed_grad_kernel(
    keep, beside, own, other, short_filter, mixed, result, conv_keep, conv_give, edge
):
    channels = result.shape[2]
    for half, query in enumerate((own, other)):
        out_grad = keep[half] + beside[1 - half].astype(F32)
        rows = turned(out_grad * query_conv(query, short_filter)).astype(BF)
        for s in range(result.shape[0]):
            result[s, lax.axis_index("zh") ^ half] = rows[s * channels : (s + 1) * channels]
        query_grad = out_grad * mixed[half].astype(F32)
        if half == 0:
            conv_keep[...] = query_grad
        else:
            conv_give[...] = query_grad.astype(BF)
        edge[half] = query_grad[:PAD].astype(BF)


def last_kernel(
    key, value, halo, beyond, short_filter, gated_grad_rows, query_own, query_other, edge_own,
    query_grad, key_grad, value_grad,
):
    tokens = query_own.shape[0]
    for which, grad, after in (
        (0, query_own[...], edge_own[:8, :]),
        (1, query_other[:tokens, :], query_other[tokens : tokens + 8, :]),
    ):
        columns = columns_of(which, grad.shape[1])
        taps = taps_of(short_filter, 0, columns)
        query_grad[:, columns] = adjoint(grad.astype(F32), after.astype(F32), taps).astype(BF)
    devices, rows, _ = gated_grad_rows.shape
    channels = rows - PAD
    count = FAST // channels
    body = turned_back(
        jnp.concatenate([gated_grad_rows[d, :channels] for d in range(devices)], axis=0)
    )
    strips = []
    for first in range(0, devices, count):
        strip = sum(gated_grad_rows[first + i, channels:].astype(F32) for i in range(count))
        strips.append(strip[:8])
    gated_grad = jnp.concatenate([body, jnp.concatenate(strips, axis=1)], axis=0)

    def conv(signal, number, branch):
        before = halo[branch * PAD : (branch + 1) * PAD, :].astype(F32)[PAD - 8 :]
        after = beyond[number * PAD : (number + 1) * PAD, :].astype(F32)[:8]
        joined = jnp.concatenate([before, signal[...].astype(F32), after], axis=0)
        return causal_rows(joined, taps_of(short_filter, branch))

    extent = key.shape[0]
    for result, grad, branch in (
        (key_grad, gated_grad * conv(value, 1, 2), 1),
        (value_grad, gated_grad * conv(key, 0, 1), 2),
    ):
        result[...] = adjoint(grad[:extent], grad[extent:], taps_of(short_filter, branch)).astype(BF)


def backward_kernel(cot, beside, weight, keep, give, both, total):
    row = pl.program_id(0)
    zh, zl, core = position("zh", "zl", "core")
    tokens, half_width = keep.shape[1:]

    @pl.when(row == 0)
    def _():
        both[0] = cot[...]
        both[1] = beside[...]
        total[...] = jnp.zeros_like(total)

    which, k1 = (row % 2) ^ core, (row // 2) ^ (zl % 2)
    lines = jnp.concatenate(
        [both[which, (half ^ zh ^ (zl // 2)) * 2 + k1] for half in range(2)], axis=0
    )
    across = (((1,), (1,)), ((), ()))
    for part in range(2):
        here = slice(part * half_width, (part + 1) * half_width)
        rows = jnp.concatenate([weight[i, here, :] for i in range(4)], axis=1)
        total[part] += lax.dot_general(lines, rows, across, preferred_element_type=F32)

    @pl.when(row == 3)
    def _():
        for half in range(2):
            here = slice(half * tokens, (half + 1) * tokens)
            keep[half] = total[zh, here, :]
            give[half] = total[1 - zh, here, :].astype(BF)


def forward_kernel(product, beside, weight, result):
    zh = lax.axis_index("zh")
    tokens = product.shape[1]
    own = jnp.concatenate([product[0], product[1]], axis=0)
    other = jnp.concatenate([beside[1], beside[0]], axis=0)
    left = jnp.concatenate(
        [jnp.where(zh == 0, own, other), jnp.where(zh == 0, other, own)], axis=1
    )
    rows = jnp.concatenate([weight[i] for i in range(4)], axis=1)
    term = jnp.dot(left, rows, preferred_element_type=F32).astype(BF)
    for half in range(2):
        result[half ^ zh, 0] = term[half * tokens : (half + 1) * tokens]


def swap(value, axis):
    return lax.ppermute(value, axis, [(0, 1), (1, 0)])


def exchange(value):
    return lax.all_to_all(value, ("y", "x"), split_axis=0, concat_axis=0, tiled=True)


def once(value, *others):
    return lax.optimization_barrier((value,) + others)[0]


def shards(query, key, value, short_filter, long_filter, out_weight, cotangent):
    tokens, width = query.shape
    seq_count = lax.axis_size(SEQ)
    length = tokens * seq_count
    channels = width // seq_count
    first_in, first_out, twist, second_in, second_out = (jnp.asarray(t) for t in tables(length))
    spec_type = shape_of((channels * length // FAST, 2 * FAST), F32)
    rows_type = shape_of((length // FAST * channels, FAST), BF)
    tokens_bf, tokens_f32 = shape_of((tokens, width), BF), shape_of((tokens, width), F32)
    held = pltpu.VMEM(rows_type.shape, F32)

    half = width // 2
    split_type = shape_of((16, 2, channels, FAST), BF)
    halves_bf = shape_of((2, tokens, half), BF)
    halves_f32 = shape_of((2, tokens, half), F32)

    weight = lax.all_gather(out_weight, ("y", "x"))

    def links(k1, k2, back):
        result = []
        for a in range(2):
            for u in range(2):
                for v in range(2):
                    chip, owner = a * 4 + u * 2 + v, (u ^ k2) * 4 + a * 2 + (v ^ k1)
                    result.append((chip, owner) if back else (owner, chip))
        return result


    last_rows = pl.BlockSpec((PAD, width), lambda *_: (tokens // PAD - 1, 0))
    halo = call(
        halo_kernel, shape_of((3 * PAD, width), BF), [], query, key, value,
        grid=(1,), specs={i: last_rows for i in range(3)},
    )
    halo = lax.ppermute(halo, SEQ, [(i, i + 1) for i in range(seq_count - 1)])
    back = [(i + 1, i) for i in range(seq_count - 1)]
    filter_spec = call(filter_kernel, spec_type, [held], long_filter, first_in, twist, second_in)
    halo = once(halo, filter_spec)
    gated_rows = call(gated_kernel, rows_type, [], key, value, halo, short_filter)
    gated_rows = lax.all_to_all(gated_rows, SEQ, split_axis=0, concat_axis=0, tiled=True)

    query_type = shape_of((PAD + tokens, half), BF)
    query_own, query_other = call(
        query_split_kernel, (query_type, query_type), [], query, halo
    )
    query_other = swap(query_other, "zh")

    beyond = lax.ppermute(jnp.concatenate([key[:PAD], value[:PAD]], axis=0), SEQ, back)

    cot_there = once(cotangent, gated_rows)
    blocks = [
        lax.ppermute(cot_there, ("zh", "zl"), links(k1, k2, False)) for k2 in range(2) for k1 in range(2)
    ]
    gated_rows = once(gated_rows, query_other)
    mixed_rows, gated_spec = call(
        functools.partial(convolve_kernel, False), (split_type, spec_type), [held, held],
        gated_rows, filter_spec, first_in, first_out, twist, second_in, second_out,
    )
    mixed_rows = exchange(mixed_rows)
    product, mixed = call(
        product_kernel, (halves_bf, halves_bf), [],
        query_own, query_other, short_filter, once(mixed_rows, beyond),
    )
    product_beside = swap(product, "zh")
    got = jnp.stack(once(tuple(blocks), product))
    got_beside = swap(got, "core")

    four = pl.BlockSpec((4,) + out_weight.shape, lambda row: (row, 0, 0))
    grads, grads_beside = call(
        backward_kernel, (halves_f32, halves_bf),
        [pltpu.VMEM((2, 4, tokens, width), BF), pltpu.VMEM((2, 2 * tokens, half), F32)],
        got, got_beside, weight, grid=(4,), specs={2: four},
    )
    product_beside = once(product_beside, grads_beside)
    grads_beside = swap(grads_beside, "zh")

    partial = call(
        forward_kernel, shape_of((2, 4, tokens, width), BF), [],
        product, product_beside, weight, grid=(4,), specs={2: four}, flops=1 << 34,
        out_specs=pl.BlockSpec((2, 1, tokens, width), lambda row: (0, row, 0, 0)),
    )
    summed = lax.psum_scatter(partial.reshape(8, tokens, width), CHAN, scatter_dimension=0)

    mixed_grad_rows, query_conv_own, query_conv_other, query_edge = call(
        mixed_grad_kernel, (split_type, shape_of((tokens, half), F32), shape_of((tokens, half), BF), shape_of((2, PAD, half), BF)), [],
        grads, once(grads_beside, partial), query_own, query_other, short_filter, mixed, flops=1 << 33,
    )
    query_edge = lax.ppermute(query_edge, ("y", "x"), [((i + 1) % 16, i) for i in range(16)])
    zh, y, x = position("zh", "y", "x")
    last = (y == 3) & (x == 3)
    zero = jnp.zeros_like(query_edge[0])
    edge_own = jnp.where(last, jnp.where(zh == 0, query_edge[1], zero), query_edge[0])
    edge_other = jnp.where(last, jnp.where(zh == 0, zero, query_edge[0]), query_edge[1])
    query_conv_other = swap(jnp.concatenate([query_conv_other, edge_other], axis=0), "zh")
    mixed_grad_rows = exchange(mixed_grad_rows)
    gated_grad_rows, mixed_spec = call(
        functools.partial(convolve_kernel, True), (shape_of((seq_count, channels + PAD, FAST), BF), spec_type), [held, held],
        mixed_grad_rows, filter_spec, first_in, first_out, twist, second_in, second_out,
        flops=1 << 35,
    )
    gated_grad_rows = lax.all_to_all(
        once(gated_grad_rows, query_conv_other), SEQ, split_axis=0, concat_axis=0, tiled=True
    )
    block_output = lax.ppermute(summed, ("zh", "zl"), links(0, 0, True))
    query_grad, key_grad, value_grad = call(
        last_kernel, (tokens_bf, tokens_bf, tokens_bf), [], key, value, halo, beyond, short_filter,
        gated_grad_rows, query_conv_own, query_conv_other, edge_own,
    )
    filter_grad = call(
        filter_grad_kernel, shape_of((channels, length), F32), [held],
        once(mixed_spec, key_grad), gated_spec, first_out, twist, second_out,
    )
    return (block_output, query_grad, key_grad, value_grad, filter_grad)


def solution(mesh):
    fine = Mesh(mesh.devices.reshape(2, 4, 4, 4, 2), SEQ + CHAN)
    return jax.shard_map(
        shards,
        mesh=fine,
        in_specs=(
            P(SEQ, CHAN),
            P(SEQ, CHAN),
            P(SEQ, CHAN),
            P(None, None, CHAN),
            P(CHAN + SEQ, None),
            P(CHAN, SEQ),
            P(SEQ, CHAN),
        ),
        out_specs=(
            P(SEQ, CHAN),
            P(SEQ, CHAN),
            P(SEQ, CHAN),
            P(SEQ, CHAN),
            P(CHAN + SEQ, None),
        ),
        check_vma=False,
    )
```

```python
import functools
import math

import jax
import jax.numpy as jnp
import numpy as np
from jax import lax
from jax.experimental import pallas as pl
from jax.experimental.pallas import tpu as pltpu
from jax.sharding import Mesh
from jax.sharding import PartitionSpec as P

SEQ = ("zh", "y", "x")
CHAN = ("zl", "core")
BF = jnp.bfloat16
F32 = jnp.float32
FAST = 128
GROUP = 8
VMEM = 65408 * 1024


def halves(value):
    high = np.asarray(value, np.float64).astype(jnp.bfloat16)
    low = (np.asarray(value, np.float64) - high.astype(np.float64)).astype(jnp.bfloat16)
    return high, low


def tables(length):
    rows = length // FAST
    slow = np.arange(rows)
    fast = np.arange(FAST)
    angle = 2 * math.pi * np.outer(slow + 0.25, slow) / rows
    first = np.concatenate([np.cos(angle), -np.sin(angle)], axis=0)
    high, low = halves(first)
    first_in = np.concatenate([high, low, high], axis=1)
    back = np.concatenate([np.cos(angle.T), -np.sin(angle.T)], axis=1) / length
    high, low = halves(back)
    first_out = np.concatenate([high, low, high], axis=1)
    twist = 2 * math.pi * np.outer(slow + 0.25, fast) / length
    twist = np.stack([np.cos(twist), np.sin(twist)]).astype(np.float32)
    turn = 2 * math.pi * np.outer(fast, fast) / FAST
    cos, sin = np.cos(turn), np.sin(turn)
    second_in = np.stack(halves(np.block([[cos, -sin], [sin, cos]])))
    second_out = np.stack(halves(np.block([[cos, sin], [-sin, cos]])))
    return first_in, first_out, twist, second_in, second_out


def split(value):
    high = value.astype(BF)
    return high, (value - high.astype(F32)).astype(BF)


def dot(first, second):
    return jnp.dot(first, second, preferred_element_type=F32)


def dot_wide(value, table):
    high, low = split(value)
    return dot(high, table[0]) + (dot(low, table[0]) + dot(high, table[1]))


def group_forward(held, group, first_in, twist, second_in):
    rows = twist.shape[1]
    channels = held.shape[0] // rows
    signal = jnp.concatenate(
        [held[pl.ds(group * GROUP + i, rows, stride=channels), :] for i in range(GROUP)], axis=1
    )
    high, low = split(signal)
    first = dot(first_in[...], jnp.concatenate([high, high, low], axis=0))
    cos, sin = twist[0], twist[1]
    parts = []
    for i in range(GROUP):
        real = first[:rows, i * FAST : (i + 1) * FAST]
        imag = first[rows:, i * FAST : (i + 1) * FAST]
        parts.append(jnp.concatenate([real * cos + imag * sin, imag * cos - real * sin], axis=1))
    return dot_wide(jnp.concatenate(parts, axis=0), second_in)


def group_inverse(spectrum, group, first_out, twist, second_out, held):
    rows = twist.shape[1]
    channels = held.shape[0] // rows
    back = dot_wide(spectrum, second_out)
    cos, sin = twist[0], twist[1]
    real_parts, imag_parts = [], []
    for i in range(GROUP):
        real = back[i * rows : (i + 1) * rows, :FAST]
        imag = back[i * rows : (i + 1) * rows, FAST:]
        real_parts.append(real * cos - imag * sin)
        imag_parts.append(real * sin + imag * cos)
    turned = jnp.concatenate(
        [jnp.concatenate(real_parts, axis=1), jnp.concatenate(imag_parts, axis=1)], axis=0
    )
    high, low = split(turned)
    result = dot(first_out[...], jnp.concatenate([high, high, low], axis=0))
    for i in range(GROUP):
        held[pl.ds(group * GROUP + i, rows, stride=channels), :] = result[:, i * FAST : (i + 1) * FAST]


def product_of(first, second, conjugate):
    first_re, first_im = first[:, :FAST], first[:, FAST:]
    second_re, second_im = second[:, :FAST], second[:, FAST:]
    if conjugate:
        return jnp.concatenate(
            [
                first_re * second_re + first_im * second_im,
                first_im * second_re - first_re * second_im,
            ],
            axis=1,
        )
    return jnp.concatenate(
        [
            first_re * second_re - first_im * second_im,
            first_re * second_im + first_im * second_re,
        ],
        axis=1,
    )


def filter_kernel(signal, first_in, twist, second_in, spectrum, held):
    rows = twist.shape[1]
    channels = signal.shape[0]
    for n1 in range(rows):
        held[n1 * channels : (n1 + 1) * channels, :] = signal[:, n1 * FAST : (n1 + 1) * FAST]
    step = GROUP * rows
    for group in range(channels // GROUP):
        spectrum[group * step : (group + 1) * step, :] = group_forward(
            held, group, first_in, twist, second_in
        )


def convolve_kernel(
    conjugate, signal, filter_spec, first_in, first_out, twist, second_in, second_out,
    result, spectrum, held, out,
):
    rows = twist.shape[1]
    channels = held.shape[0] // rows
    step = GROUP * rows

    def line(n1):
        return slice(n1 * channels, (n1 + 1) * channels)

    if len(signal.shape) == 2:
        held[...] = signal[...].astype(F32)
    else:
        for n1 in range(rows):
            held[line(n1), :] = signal[n1 % signal.shape[0], n1 // signal.shape[0]].astype(F32)
    for group in range(channels // GROUP):
        here = slice(group * step, (group + 1) * step)
        spec = group_forward(held, group, first_in, twist, second_in)
        spectrum[here, :] = spec
        both = product_of(spec, filter_spec[here, :], conjugate)
        group_inverse(both, group, first_out, twist, second_out, out)
    if len(result.shape) == 4:
        for n1 in range(rows):
            result[n1 % result.shape[0], n1 // result.shape[0]] = out[line(n1), :].astype(result.dtype)
        return
    count = FAST // channels
    place = lax.axis_index("x")
    column = lax.broadcasted_iota(jnp.int32, (8, FAST), 1)
    mine = (column >= place * channels) & (column < (place + 1) * channels)
    empty = jnp.zeros((PAD - 8, FAST), F32)
    for n1 in range(rows):
        result[n1, :channels] = out[line(n1), :].astype(result.dtype)
        if n1 % count == 0:
            ahead = out[n1 * channels : (n1 + count) * channels, :].T[:8]
        if n1 > 0:
            moved = pltpu.roll(ahead, (place + 4 - n1 % count) % 4 * channels, 1)
            strip = jnp.concatenate([jnp.where(mine, moved, 0.0), empty], axis=0)
            result[n1 - 1, channels:] = strip.astype(result.dtype)
    result[rows - 1, channels:] = jnp.zeros((PAD, FAST), result.dtype)


def filter_grad_kernel(first_spec, second_spec, first_out, twist, second_out, result, out):
    rows = twist.shape[1]
    channels = result.shape[0]
    scale = result.shape[1] ** -0.5
    step = GROUP * rows
    for group in range(channels // GROUP):
        here = slice(group * step, (group + 1) * step)
        both = product_of(first_spec[here, :], second_spec[here, :], True) * scale
        group_inverse(both, group, first_out, twist, second_out, out)
    for n1 in range(rows):
        result[:, n1 * FAST : (n1 + 1) * FAST] = out[n1 * channels : (n1 + 1) * channels, :]


def whole(array):
    return pl.BlockSpec(array.shape, lambda *_: (0,) * len(array.shape))


def call(kernel, out_shape, scratch, *args, grid=(), specs=None, out_specs=None, flops=1024):
    specs = specs or {}
    return pl.pallas_call(
        kernel,
        out_shape=out_shape,
        grid=grid,
        in_specs=[specs.get(i, whole(arg)) for i, arg in enumerate(args)],
        out_specs=out_specs or jax.tree.map(whole, out_shape),
        scratch_shapes=scratch,
        compiler_params=pltpu.CompilerParams(vmem_limit_bytes=VMEM),
        cost_estimate=pl.CostEstimate(flops=flops, bytes_accessed=1024, transcendentals=0),
    )(*args)


def position(*names):
    return tuple(lax.axis_index(name) for name in names)


def shape_of(dims, dtype):
    return jax.ShapeDtypeStruct(dims, dtype)


PAD = 16


def taps_of(short_filter, branch, columns=slice(None)):
    return [short_filter[tap, branch : branch + 1, columns] for tap in range(3)]


def causal_rows(joined, taps):
    extent = joined.shape[0] - 8
    return (
        taps[0] * joined[8:] + taps[1] * joined[7 : 7 + extent] + taps[2] * joined[6 : 6 + extent]
    )


def causal(signal, halo, short_filter, branch):
    before = halo[branch * PAD : (branch + 1) * PAD, :].astype(F32)[PAD - 8 :]
    joined = jnp.concatenate([before, signal[...].astype(F32)], axis=0)
    return causal_rows(joined, taps_of(short_filter, branch))


def adjoint(signal, after, taps):
    extent = signal.shape[0]
    joined = jnp.concatenate([signal, after], axis=0)
    return (
        taps[0] * joined[:extent]
        + taps[1] * joined[1 : extent + 1]
        + taps[2] * joined[2 : extent + 2]
    )


def turned(value):
    return jnp.concatenate(
        [value[:, i : i + 128].T for i in range(0, value.shape[1], 128)], axis=0
    )


def turned_back(rows):
    rows = rows.astype(F32)
    return jnp.concatenate(
        [rows[i : i + 128].T for i in range(0, rows.shape[0], 128)], axis=1
    )


def gated_kernel(key, value, halo, short_filter, result):
    gated = causal(key, halo, short_filter, 1) * causal(value, halo, short_filter, 2)
    result[...] = turned(gated).astype(BF)


def columns_of(which, width):
    return pl.ds(pl.multiple_of((lax.axis_index("zh") ^ which) * width, width), width)


def halo_kernel(query, key, value, result):
    for branch, ref in enumerate((query, key, value)):
        result[branch * PAD : (branch + 1) * PAD, :] = ref[...]


def query_split_kernel(query, halo, keep, give):
    for which, result in ((0, keep), (1, give)):
        columns = columns_of(which, result.shape[1])
        result[:PAD, :] = halo[:PAD, columns]
        result[PAD:, :] = query[:, columns]


def query_conv(query, short_filter):
    taps = taps_of(short_filter, 0, columns_of(0, query.shape[1]))
    return causal_rows(query[...].astype(F32)[PAD - 8 :], taps)


def product_kernel(own, other, short_filter, mixed_rows, product, mixed):
    for half, query in enumerate((own, other)):
        there = lax.axis_index("zh") ^ half
        sources, _, channels, _ = mixed_rows.shape
        blocks = []
        for first in range(0, sources * channels, 128):
            rows = [
                mixed_rows[s, there] for s in range(first // channels, (first + 128) // channels)
            ]
            blocks.append(jnp.concatenate(rows, axis=0).astype(F32).T)
        here = jnp.concatenate(blocks, axis=1)
        mixed[half] = here.astype(BF)
        product[half] = (query_conv(query, short_filter) * here).astype(BF)


def mixed_grad_kernel(
    keep, beside, own, other, short_filter, mixed, result, conv_keep, conv_give, edge
):
    channels = result.shape[2]
    for half, query in enumerate((own, other)):
        out_grad = keep[half] + beside[1 - half].astype(F32)
        rows = turned(out_grad * query_conv(query, short_filter)).astype(BF)
        for s in range(result.shape[0]):
            result[s, lax.axis_index("zh") ^ half] = rows[s * channels : (s + 1) * channels]
        query_grad = out_grad * mixed[half].astype(F32)
        if half == 0:
            conv_keep[...] = query_grad
        else:
            conv_give[...] = query_grad.astype(BF)
        edge[half] = query_grad[:PAD].astype(BF)


def last_kernel(
    key, value, halo, beyond, short_filter, gated_grad_rows, query_own, query_other, edge_own,
    query_grad, key_grad, value_grad,
):
    tokens = query_own.shape[0]
    for which, grad, after in (
        (0, query_own[...], edge_own[:8, :]),
        (1, query_other[:tokens, :], query_other[tokens : tokens + 8, :]),
    ):
        columns = columns_of(which, grad.shape[1])
        taps = taps_of(short_filter, 0, columns)
        query_grad[:, columns] = adjoint(grad.astype(F32), after.astype(F32), taps).astype(BF)
    devices, rows, _ = gated_grad_rows.shape
    channels = rows - PAD
    count = FAST // channels
    body = turned_back(
        jnp.concatenate([gated_grad_rows[d, :channels] for d in range(devices)], axis=0)
    )
    strips = []
    for first in range(0, devices, count):
        strip = sum(gated_grad_rows[first + i, channels:].astype(F32) for i in range(count))
        strips.append(strip[:8])
    gated_grad = jnp.concatenate([body, jnp.concatenate(strips, axis=1)], axis=0)

    def conv(signal, number, branch):
        before = halo[branch * PAD : (branch + 1) * PAD, :].astype(F32)[PAD - 8 :]
        after = beyond[number * PAD : (number + 1) * PAD, :].astype(F32)[:8]
        joined = jnp.concatenate([before, signal[...].astype(F32), after], axis=0)
        return causal_rows(joined, taps_of(short_filter, branch))

    extent = key.shape[0]
    for result, grad, branch in (
        (key_grad, gated_grad * conv(value, 1, 2), 1),
        (value_grad, gated_grad * conv(key, 0, 1), 2),
    ):
        result[...] = adjoint(grad[:extent], grad[extent:], taps_of(short_filter, branch)).astype(BF)


def backward_kernel(cot, beside, weight, keep, give, both, total):
    row = pl.program_id(0)
    zh, zl, core = position("zh", "zl", "core")
    tokens, half_width = keep.shape[1:]

    @pl.when(row == 0)
    def _():
        both[0] = cot[...]
        both[1] = beside[...]
        total[...] = jnp.zeros_like(total)

    which, k1 = (row % 2) ^ core, (row // 2) ^ (zl % 2)
    lines = jnp.concatenate(
        [both[which, (half ^ zh ^ (zl // 2)) * 2 + k1] for half in range(2)], axis=0
    )
    across = (((1,), (1,)), ((), ()))
    for part in range(2):
        here = slice(part * half_width, (part + 1) * half_width)
        rows = jnp.concatenate([weight[i, here, :] for i in range(4)], axis=1)
        total[part] += lax.dot_general(lines, rows, across, preferred_element_type=F32)

    @pl.when(row == 3)
    def _():
        for half in range(2):
            here = slice(half * tokens, (half + 1) * tokens)
            keep[half] = total[zh, here, :]
            give[half] = total[1 - zh, here, :].astype(BF)


def forward_kernel(product, beside, weight, result):
    zh = lax.axis_index("zh")
    tokens = product.shape[1]
    own = jnp.concatenate([product[0], product[1]], axis=0)
    other = jnp.concatenate([beside[1], beside[0]], axis=0)
    left = jnp.concatenate(
        [jnp.where(zh == 0, own, other), jnp.where(zh == 0, other, own)], axis=1
    )
    rows = jnp.concatenate([weight[i] for i in range(4)], axis=1)
    term = jnp.dot(left, rows, preferred_element_type=F32).astype(BF)
    for half in range(2):
        result[half ^ zh, 0] = term[half * tokens : (half + 1) * tokens]


def swap(value, axis):
    return lax.ppermute(value, axis, [(0, 1), (1, 0)])


def exchange(value):
    return lax.all_to_all(value, ("y", "x"), split_axis=0, concat_axis=0, tiled=True)


def once(value, *others):
    return lax.optimization_barrier((value,) + others)[0]


def shards(query, key, value, short_filter, long_filter, out_weight, cotangent):
    tokens, width = query.shape
    seq_count = lax.axis_size(SEQ)
    length = tokens * seq_count
    channels = width // seq_count
    first_in, first_out, twist, second_in, second_out = (jnp.asarray(t) for t in tables(length))
    spec_type = shape_of((channels * length // FAST, 2 * FAST), F32)
    rows_type = shape_of((length // FAST * channels, FAST), BF)
    tokens_bf, tokens_f32 = shape_of((tokens, width), BF), shape_of((tokens, width), F32)
    held = pltpu.VMEM(rows_type.shape, F32)

    half = width // 2
    split_type = shape_of((16, 2, channels, FAST), BF)
    halves_bf = shape_of((2, tokens, half), BF)
    halves_f32 = shape_of((2, tokens, half), F32)

    weight = lax.all_gather(out_weight, ("y", "x"))

    def links(k1, k2, back):
        result = []
        for a in range(2):
            for u in range(2):
                for v in range(2):
                    chip, owner = a * 4 + u * 2 + v, (u ^ k2) * 4 + a * 2 + (v ^ k1)
                    result.append((chip, owner) if back else (owner, chip))
        return result


    last_rows = pl.BlockSpec((PAD, width), lambda *_: (tokens // PAD - 1, 0))
    halo = call(
        halo_kernel, shape_of((3 * PAD, width), BF), [], query, key, value,
        grid=(1,), specs={i: last_rows for i in range(3)},
    )
    halo = lax.ppermute(halo, SEQ, [(i, i + 1) for i in range(seq_count - 1)])
    back = [(i + 1, i) for i in range(seq_count - 1)]
    filter_spec = call(filter_kernel, spec_type, [held], long_filter, first_in, twist, second_in)
    halo = once(halo, filter_spec)
    gated_rows = call(gated_kernel, rows_type, [], key, value, halo, short_filter)
    gated_rows = lax.all_to_all(gated_rows, SEQ, split_axis=0, concat_axis=0, tiled=True)

    query_type = shape_of((PAD + tokens, half), BF)
    query_own, query_other = call(
        query_split_kernel, (query_type, query_type), [], query, halo
    )
    query_other = swap(query_other, "zh")

    beyond = lax.ppermute(jnp.concatenate([key[:PAD], value[:PAD]], axis=0), SEQ, back)

    cot_there = once(cotangent, gated_rows)
    blocks = [
        lax.ppermute(cot_there, ("zh", "zl"), links(k1, k2, False)) for k2 in range(2) for k1 in range(2)
    ]
    gated_rows = once(gated_rows, query_other)
    mixed_rows, gated_spec = call(
        functools.partial(convolve_kernel, False), (split_type, spec_type), [held, held],
        gated_rows, filter_spec, first_in, first_out, twist, second_in, second_out,
    )
    mixed_rows = exchange(mixed_rows)
    product, mixed = call(
        product_kernel, (halves_bf, halves_bf), [],
        query_own, query_other, short_filter, once(mixed_rows, beyond),
    )
    product_beside = swap(product, "zh")
    got = jnp.stack(once(tuple(blocks), product))
    got_beside = swap(got, "core")

    four = pl.BlockSpec((4,) + out_weight.shape, lambda row: (row, 0, 0))
    grads, grads_beside = call(
        backward_kernel, (halves_f32, halves_bf),
        [pltpu.VMEM((2, 4, tokens, width), BF), pltpu.VMEM((2, 2 * tokens, half), F32)],
        got, got_beside, weight, grid=(4,), specs={2: four},
    )
    product_beside = once(product_beside, grads_beside)
    grads_beside = swap(grads_beside, "zh")

    partial = call(
        forward_kernel, shape_of((2, 4, tokens, width), BF), [],
        product, product_beside, weight, grid=(4,), specs={2: four}, flops=1 << 34,
        out_specs=pl.BlockSpec((2, 1, tokens, width), lambda row: (0, row, 0, 0)),
    )
    summed = lax.psum_scatter(partial.reshape(8, tokens, width), CHAN, scatter_dimension=0)

    mixed_grad_rows, query_conv_own, query_conv_other, query_edge = call(
        mixed_grad_kernel, (split_type, shape_of((tokens, half), F32), shape_of((tokens, half), BF), shape_of((2, PAD, half), BF)), [],
        grads, once(grads_beside, partial), query_own, query_other, short_filter, mixed, flops=1 << 33,
    )
    query_edge = lax.ppermute(query_edge, ("y", "x"), [((i + 1) % 16, i) for i in range(16)])
    zh, y, x = position("zh", "y", "x")
    last = (y == 3) & (x == 3)
    zero = jnp.zeros_like(query_edge[0])
    edge_own = jnp.where(last, jnp.where(zh == 0, query_edge[1], zero), query_edge[0])
    edge_other = jnp.where(last, jnp.where(zh == 0, zero, query_edge[0]), query_edge[1])
    query_conv_other = swap(jnp.concatenate([query_conv_other, edge_other], axis=0), "zh")
    mixed_grad_rows = exchange(mixed_grad_rows)
    gated_grad_rows, mixed_spec = call(
        functools.partial(convolve_kernel, True), (shape_of((seq_count, channels + PAD, FAST), BF), spec_type), [held, held],
        mixed_grad_rows, filter_spec, first_in, first_out, twist, second_in, second_out,
        flops=1 << 35,
    )
    gated_grad_rows = lax.all_to_all(
        once(gated_grad_rows, query_conv_other), SEQ, split_axis=0, concat_axis=0, tiled=True
    )
    block_output = lax.ppermute(summed, ("zh", "zl"), links(0, 0, True))
    filter_grad = call(
        filter_grad_kernel, shape_of((channels, length), F32), [held],
        mixed_spec, gated_spec, first_out, twist, second_out,
    )
    query_grad, key_grad, value_grad = call(
        last_kernel, (tokens_bf, tokens_bf, tokens_bf), [], key, value, halo, beyond, short_filter,
        once(gated_grad_rows, filter_grad), query_conv_own, query_conv_other, edge_own,
    )
    return (block_output, query_grad, key_grad, value_grad, filter_grad)


def solution(mesh):
    fine = Mesh(mesh.devices.reshape(2, 4, 4, 4, 2), SEQ + CHAN)
    return jax.shard_map(
        shards,
        mesh=fine,
        in_specs=(
            P(SEQ, CHAN),
            P(SEQ, CHAN),
            P(SEQ, CHAN),
            P(None, None, CHAN),
            P(CHAN + SEQ, None),
            P(CHAN, SEQ),
            P(SEQ, CHAN),
        ),
        out_specs=(
            P(SEQ, CHAN),
            P(SEQ, CHAN),
            P(SEQ, CHAN),
            P(SEQ, CHAN),
            P(CHAN + SEQ, None),
        ),
        check_vma=False,
    )
```

```python
import functools
import math

import jax
import jax.numpy as jnp
import numpy as np
from jax import lax
from jax.experimental import pallas as pl
from jax.experimental.pallas import tpu as pltpu
from jax.sharding import Mesh
from jax.sharding import PartitionSpec as P

SEQ = ("zh", "y", "x")
CHAN = ("zl", "core")
BF = jnp.bfloat16
F32 = jnp.float32
FAST = 128
GROUP = 8
VMEM = 65408 * 1024


def halves(value):
    high = np.asarray(value, np.float64).astype(jnp.bfloat16)
    low = (np.asarray(value, np.float64) - high.astype(np.float64)).astype(jnp.bfloat16)
    return high, low


def tables(length):
    rows = length // FAST
    slow = np.arange(rows)
    fast = np.arange(FAST)
    angle = 2 * math.pi * np.outer(slow + 0.25, slow) / rows
    first = np.concatenate([np.cos(angle), -np.sin(angle)], axis=0)
    high, low = halves(first)
    first_in = np.concatenate([high, low, high], axis=1)
    back = np.concatenate([np.cos(angle.T), -np.sin(angle.T)], axis=1) / length
    high, low = halves(back)
    first_out = np.concatenate([high, low, high], axis=1)
    twist = 2 * math.pi * np.outer(slow + 0.25, fast) / length
    twist = np.stack([np.cos(twist), np.sin(twist)]).astype(np.float32)
    turn = 2 * math.pi * np.outer(fast, fast) / FAST
    cos, sin = np.cos(turn), np.sin(turn)
    second_in = np.stack(halves(np.block([[cos, -sin], [sin, cos]])))
    second_out = np.stack(halves(np.block([[cos, sin], [-sin, cos]])))
    return first_in, first_out, twist, second_in, second_out


def split(value):
    high = value.astype(BF)
    return high, (value - high.astype(F32)).astype(BF)


def dot(first, second):
    return jnp.dot(first, second, preferred_element_type=F32)


def dot_wide(value, table):
    high, low = split(value)
    return dot(high, table[0]) + (dot(low, table[0]) + dot(high, table[1]))


def group_forward(held, group, first_in, twist, second_in):
    rows = twist.shape[1]
    channels = held.shape[0] // rows
    signal = jnp.concatenate(
        [held[pl.ds(group * GROUP + i, rows, stride=channels), :] for i in range(GROUP)], axis=1
    )
    high, low = split(signal)
    first = dot(first_in[...], jnp.concatenate([high, high, low], axis=0))
    cos, sin = twist[0], twist[1]
    parts = []
    for i in range(GROUP):
        real = first[:rows, i * FAST : (i + 1) * FAST]
        imag = first[rows:, i * FAST : (i + 1) * FAST]
        parts.append(jnp.concatenate([real * cos + imag * sin, imag * cos - real * sin], axis=1))
    return dot_wide(jnp.concatenate(parts, axis=0), second_in)


def group_inverse(spectrum, group, first_out, twist, second_out, held):
    rows = twist.shape[1]
    channels = held.shape[0] // rows
    back = dot_wide(spectrum, second_out)
    cos, sin = twist[0], twist[1]
    real_parts, imag_parts = [], []
    for i in range(GROUP):
        real = back[i * rows : (i + 1) * rows, :FAST]
        imag = back[i * rows : (i + 1) * rows, FAST:]
        real_parts.append(real * cos - imag * sin)
        imag_parts.append(real * sin + imag * cos)
    turned = jnp.concatenate(
        [jnp.concatenate(real_parts, axis=1), jnp.concatenate(imag_parts, axis=1)], axis=0
    )
    high, low = split(turned)
    result = dot(first_out[...], jnp.concatenate([high, high, low], axis=0))
    for i in range(GROUP):
        held[pl.ds(group * GROUP + i, rows, stride=channels), :] = result[:, i * FAST : (i + 1) * FAST]


def product_of(first, second, conjugate):
    first_re, first_im = first[:, :FAST], first[:, FAST:]
    second_re, second_im = second[:, :FAST], second[:, FAST:]
    if conjugate:
        return jnp.concatenate(
            [
                first_re * second_re + first_im * second_im,
                first_im * second_re - first_re * second_im,
            ],
            axis=1,
        )
    return jnp.concatenate(
        [
            first_re * second_re - first_im * second_im,
            first_re * second_im + first_im * second_re,
        ],
        axis=1,
    )


def filter_kernel(signal, first_in, twist, second_in, spectrum, held):
    rows = twist.shape[1]
    channels = signal.shape[0]
    for n1 in range(rows):
        held[n1 * channels : (n1 + 1) * channels, :] = signal[:, n1 * FAST : (n1 + 1) * FAST]
    step = GROUP * rows
    for group in range(channels // GROUP):
        spectrum[group * step : (group + 1) * step, :] = group_forward(
            held, group, first_in, twist, second_in
        )


def convolve_kernel(
    conjugate, signal, filter_spec, first_in, first_out, twist, second_in, second_out,
    result, spectrum, held, out,
):
    rows = twist.shape[1]
    channels = held.shape[0] // rows
    step = GROUP * rows

    def line(n1):
        return slice(n1 * channels, (n1 + 1) * channels)

    if len(signal.shape) == 2:
        held[...] = signal[...].astype(F32)
    else:
        for n1 in range(rows):
            held[line(n1), :] = signal[n1 % signal.shape[0], n1 // signal.shape[0]].astype(F32)
    for group in range(channels // GROUP):
        here = slice(group * step, (group + 1) * step)
        spec = group_forward(held, group, first_in, twist, second_in)
        spectrum[here, :] = spec
        both = product_of(spec, filter_spec[here, :], conjugate)
        group_inverse(both, group, first_out, twist, second_out, out)
    if len(result.shape) == 4:
        for n1 in range(rows):
            result[n1 % result.shape[0], n1 // result.shape[0]] = out[line(n1), :].astype(result.dtype)
        return
    count = FAST // channels
    place = lax.axis_index("x")
    column = lax.broadcasted_iota(jnp.int32, (8, FAST), 1)
    mine = (column >= place * channels) & (column < (place + 1) * channels)
    empty = jnp.zeros((PAD - 8, FAST), F32)
    for n1 in range(rows):
        result[n1, :channels] = out[line(n1), :].astype(result.dtype)
        if n1 % count == 0:
            ahead = out[n1 * channels : (n1 + count) * channels, :].T[:8]
        if n1 > 0:
            moved = pltpu.roll(ahead, (place + 4 - n1 % count) % 4 * channels, 1)
            strip = jnp.concatenate([jnp.where(mine, moved, 0.0), empty], axis=0)
            result[n1 - 1, channels:] = strip.astype(result.dtype)
    result[rows - 1, channels:] = jnp.zeros((PAD, FAST), result.dtype)


def filter_grad_kernel(first_spec, second_spec, first_out, twist, second_out, result, out):
    rows = twist.shape[1]
    channels = result.shape[0]
    scale = result.shape[1] ** -0.5
    step = GROUP * rows
    for group in range(channels // GROUP):
        here = slice(group * step, (group + 1) * step)
        both = product_of(first_spec[here, :], second_spec[here, :], True) * scale
        group_inverse(both, group, first_out, twist, second_out, out)
    for n1 in range(rows):
        result[:, n1 * FAST : (n1 + 1) * FAST] = out[n1 * channels : (n1 + 1) * channels, :]


def whole(array):
    return pl.BlockSpec(array.shape, lambda *_: (0,) * len(array.shape))


def call(kernel, out_shape, scratch, *args, grid=(), specs=None, out_specs=None, flops=1024):
    specs = specs or {}
    return pl.pallas_call(
        kernel,
        out_shape=out_shape,
        grid=grid,
        in_specs=[specs.get(i, whole(arg)) for i, arg in enumerate(args)],
        out_specs=out_specs or jax.tree.map(whole, out_shape),
        scratch_shapes=scratch,
        compiler_params=pltpu.CompilerParams(vmem_limit_bytes=VMEM),
        cost_estimate=pl.CostEstimate(flops=flops, bytes_accessed=1024, transcendentals=0),
    )(*args)


def position(*names):
    return tuple(lax.axis_index(name) for name in names)


def shape_of(dims, dtype):
    return jax.ShapeDtypeStruct(dims, dtype)


PAD = 16


def taps_of(short_filter, branch, columns=slice(None)):
    return [short_filter[tap, branch : branch + 1, columns] for tap in range(3)]


def causal_rows(joined, taps):
    extent = joined.shape[0] - 8
    return (
        taps[0] * joined[8:] + taps[1] * joined[7 : 7 + extent] + taps[2] * joined[6 : 6 + extent]
    )


def causal(signal, halo, short_filter, branch):
    before = halo[branch * PAD : (branch + 1) * PAD, :].astype(F32)[PAD - 8 :]
    joined = jnp.concatenate([before, signal[...].astype(F32)], axis=0)
    return causal_rows(joined, taps_of(short_filter, branch))


def adjoint(signal, after, taps):
    extent = signal.shape[0]
    joined = jnp.concatenate([signal, after], axis=0)
    return (
        taps[0] * joined[:extent]
        + taps[1] * joined[1 : extent + 1]
        + taps[2] * joined[2 : extent + 2]
    )


def turned(value):
    return jnp.concatenate(
        [value[:, i : i + 128].T for i in range(0, value.shape[1], 128)], axis=0
    )


def turned_back(rows):
    rows = rows.astype(F32)
    return jnp.concatenate(
        [rows[i : i + 128].T for i in range(0, rows.shape[0], 128)], axis=1
    )


def gated_kernel(key, value, halo, short_filter, result):
    gated = causal(key, halo, short_filter, 1) * causal(value, halo, short_filter, 2)
    result[...] = turned(gated).astype(BF)


def columns_of(which, width):
    return pl.ds(pl.multiple_of((lax.axis_index("zh") ^ which) * width, width), width)


def halo_kernel(query, key, value, result):
    for branch, ref in enumerate((query, key, value)):
        result[branch * PAD : (branch + 1) * PAD, :] = ref[...]


def query_split_kernel(query, halo, keep, give):
    for which, result in ((0, keep), (1, give)):
        columns = columns_of(which, result.shape[1])
        result[:PAD, :] = halo[:PAD, columns]
        result[PAD:, :] = query[:, columns]


def query_conv(query, short_filter):
    taps = taps_of(short_filter, 0, columns_of(0, query.shape[1]))
    return causal_rows(query[...].astype(F32)[PAD - 8 :], taps)


def product_kernel(own, other, short_filter, mixed_rows, product, mixed):
    for half, query in enumerate((own, other)):
        there = lax.axis_index("zh") ^ half
        sources, _, channels, _ = mixed_rows.shape
        blocks = []
        for first in range(0, sources * channels, 128):
            rows = [
                mixed_rows[s, there] for s in range(first // channels, (first + 128) // channels)
            ]
            blocks.append(jnp.concatenate(rows, axis=0).astype(F32).T)
        here = jnp.concatenate(blocks, axis=1)
        mixed[half] = here.astype(BF)
        product[half] = (query_conv(query, short_filter) * here).astype(BF)


def mixed_grad_kernel(
    keep, beside, own, other, short_filter, mixed, result, conv_keep, conv_give, edge
):
    channels = result.shape[2]
    for half, query in enumerate((own, other)):
        out_grad = keep[half] + beside[1 - half].astype(F32)
        rows = turned(out_grad * query_conv(query, short_filter)).astype(BF)
        for s in range(result.shape[0]):
            result[s, lax.axis_index("zh") ^ half] = rows[s * channels : (s + 1) * channels]
        query_grad = out_grad * mixed[half].astype(F32)
        if half == 0:
            conv_keep[...] = query_grad
        else:
            conv_give[...] = query_grad.astype(BF)
        edge[half] = query_grad[:PAD].astype(BF)


def last_kernel(
    key, value, halo, beyond, short_filter, gated_grad_rows, query_own, query_other, edge_own,
    query_grad, key_grad, value_grad,
):
    tokens = query_own.shape[0]
    for which, grad, after in (
        (0, query_own[...], edge_own[...]),
        (1, query_other[:tokens, :], query_other[tokens:, :]),
    ):
        columns = columns_of(which, grad.shape[1])
        taps = taps_of(short_filter, 0, columns)
        query_grad[:, columns] = adjoint(grad.astype(F32), after.astype(F32), taps).astype(BF)
    devices, rows, _ = gated_grad_rows.shape
    channels = rows - PAD
    count = FAST // channels
    body = turned_back(
        jnp.concatenate([gated_grad_rows[d, :channels] for d in range(devices)], axis=0)
    )
    strips = []
    for first in range(0, devices, count):
        strip = sum(gated_grad_rows[first + i, channels:].astype(F32) for i in range(count))
        strips.append(strip[:8])
    gated_grad = jnp.concatenate([body, jnp.concatenate(strips, axis=1)], axis=0)

    def conv(signal, number, branch):
        before = halo[branch * PAD : (branch + 1) * PAD, :].astype(F32)[PAD - 8 :]
        after = beyond[number * PAD : (number + 1) * PAD, :].astype(F32)[:8]
        joined = jnp.concatenate([before, signal[...].astype(F32), after], axis=0)
        return causal_rows(joined, taps_of(short_filter, branch))

    extent = key.shape[0]
    for result, grad, branch in (
        (key_grad, gated_grad * conv(value, 1, 2), 1),
        (value_grad, gated_grad * conv(key, 0, 1), 2),
    ):
        result[...] = adjoint(grad[:extent], grad[extent:], taps_of(short_filter, branch)).astype(BF)


def backward_kernel(cot, beside, weight, keep, give, both, total):
    row = pl.program_id(0)
    zh, zl, core = position("zh", "zl", "core")
    tokens, half_width = keep.shape[1:]

    @pl.when(row == 0)
    def _():
        both[0] = cot[...]
        both[1] = beside[...]
        total[...] = jnp.zeros_like(total)

    which, k1 = (row % 2) ^ core, (row // 2) ^ (zl % 2)
    lines = jnp.concatenate(
        [both[which, (half ^ zh ^ (zl // 2)) * 2 + k1] for half in range(2)], axis=0
    )
    across = (((1,), (1,)), ((), ()))
    for part in range(2):
        here = slice(part * half_width, (part + 1) * half_width)
        rows = jnp.concatenate([weight[i, here, :] for i in range(4)], axis=1)
        total[part] += lax.dot_general(lines, rows, across, preferred_element_type=F32)

    @pl.when(row == 3)
    def _():
        for half in range(2):
            here = slice(half * tokens, (half + 1) * tokens)
            keep[half] = total[zh, here, :]
            give[half] = total[1 - zh, here, :].astype(BF)


def forward_kernel(product, beside, weight, result):
    zh = lax.axis_index("zh")
    tokens = product.shape[1]
    own = jnp.concatenate([product[0], product[1]], axis=0)
    other = jnp.concatenate([beside[1], beside[0]], axis=0)
    left = jnp.concatenate(
        [jnp.where(zh == 0, own, other), jnp.where(zh == 0, other, own)], axis=1
    )
    rows = jnp.concatenate([weight[i] for i in range(4)], axis=1)
    term = jnp.dot(left, rows, preferred_element_type=F32).astype(BF)
    for half in range(2):
        result[half ^ zh, 0] = term[half * tokens : (half + 1) * tokens]


def swap(value, axis):
    return lax.ppermute(value, axis, [(0, 1), (1, 0)])


def exchange(value):
    return lax.all_to_all(value, ("y", "x"), split_axis=0, concat_axis=0, tiled=True)


def once(value, *others):
    return lax.optimization_barrier((value,) + others)[0]


def shards(query, key, value, short_filter, long_filter, out_weight, cotangent):
    tokens, width = query.shape
    seq_count = lax.axis_size(SEQ)
    length = tokens * seq_count
    channels = width // seq_count
    first_in, first_out, twist, second_in, second_out = (jnp.asarray(t) for t in tables(length))
    spec_type = shape_of((channels * length // FAST, 2 * FAST), F32)
    rows_type = shape_of((length // FAST * channels, FAST), BF)
    tokens_bf, tokens_f32 = shape_of((tokens, width), BF), shape_of((tokens, width), F32)
    held = pltpu.VMEM(rows_type.shape, F32)

    half = width // 2
    split_type = shape_of((16, 2, channels, FAST), BF)
    halves_bf = shape_of((2, tokens, half), BF)
    halves_f32 = shape_of((2, tokens, half), F32)

    weight = lax.all_gather(out_weight, ("y", "x"))

    def links(k1, k2, back):
        result = []
        for a in range(2):
            for u in range(2):
                for v in range(2):
                    chip, owner = a * 4 + u * 2 + v, (u ^ k2) * 4 + a * 2 + (v ^ k1)
                    result.append((chip, owner) if back else (owner, chip))
        return result


    last_rows = pl.BlockSpec((PAD, width), lambda *_: (tokens // PAD - 1, 0))
    halo = call(
        halo_kernel, shape_of((3 * PAD, width), BF), [], query, key, value,
        grid=(1,), specs={i: last_rows for i in range(3)},
    )
    halo = lax.ppermute(halo, SEQ, [(i, i + 1) for i in range(seq_count - 1)])
    back = [(i + 1, i) for i in range(seq_count - 1)]
    filter_spec = call(filter_kernel, spec_type, [held], long_filter, first_in, twist, second_in)
    halo = once(halo, filter_spec)
    gated_rows = call(gated_kernel, rows_type, [], key, value, halo, short_filter)
    gated_rows = lax.all_to_all(gated_rows, SEQ, split_axis=0, concat_axis=0, tiled=True)

    query_type = shape_of((PAD + tokens, half), BF)
    query_own, query_other = call(
        query_split_kernel, (query_type, query_type), [], query, halo
    )
    query_other = swap(query_other, "zh")

    beyond = lax.ppermute(jnp.concatenate([key[:PAD], value[:PAD]], axis=0), SEQ, back)

    cot_there = once(cotangent, gated_rows)
    blocks = [
        lax.ppermute(cot_there, ("zh", "zl"), links(k1, k2, False)) for k2 in range(2) for k1 in range(2)
    ]
    gated_rows = once(gated_rows, query_other)
    mixed_rows, gated_spec = call(
        functools.partial(convolve_kernel, False), (split_type, spec_type), [held, held],
        gated_rows, filter_spec, first_in, first_out, twist, second_in, second_out,
    )
    mixed_rows = exchange(mixed_rows)
    product, mixed = call(
        product_kernel, (halves_bf, halves_bf), [],
        query_own, query_other, short_filter, once(mixed_rows, beyond),
    )
    product_beside = swap(product, "zh")
    got = jnp.stack(once(tuple(blocks), product))
    got_beside = swap(got, "core")

    four = pl.BlockSpec((4,) + out_weight.shape, lambda row: (row, 0, 0))
    grads, grads_beside = call(
        backward_kernel, (halves_f32, halves_bf),
        [pltpu.VMEM((2, 4, tokens, width), BF), pltpu.VMEM((2, 2 * tokens, half), F32)],
        got, got_beside, weight, grid=(4,), specs={2: four},
    )
    product_beside = once(product_beside, grads_beside)
    grads_beside = swap(grads_beside, "zh")

    partial = call(
        forward_kernel, shape_of((2, 4, tokens, width), BF), [],
        product, product_beside, weight, grid=(4,), specs={2: four}, flops=1 << 34,
        out_specs=pl.BlockSpec((2, 1, tokens, width), lambda row: (0, row, 0, 0)),
    )
    summed = lax.psum_scatter(partial.reshape(8, tokens, width), CHAN, scatter_dimension=0)

    mixed_grad_rows, query_conv_own, query_conv_other, query_edge = call(
        mixed_grad_kernel, (split_type, shape_of((tokens, half), F32), shape_of((tokens, half), BF), shape_of((2, PAD, half), BF)), [],
        grads, once(grads_beside, partial), query_own, query_other, short_filter, mixed, flops=1 << 33,
    )
    query_edge = lax.ppermute(query_edge, ("y", "x"), [((i + 1) % 16, i) for i in range(16)])
    zh, y, x = position("zh", "y", "x")
    last = (y == 3) & (x == 3)
    zero = jnp.zeros_like(query_edge[0])
    edge_own = jnp.where(last, jnp.where(zh == 0, query_edge[1], zero), query_edge[0])
    edge_other = jnp.where(last, jnp.where(zh == 0, zero, query_edge[0]), query_edge[1])
    query_conv_other = swap(jnp.concatenate([query_conv_other, edge_other], axis=0), "zh")
    mixed_grad_rows = exchange(mixed_grad_rows)
    gated_grad_rows, mixed_spec = call(
        functools.partial(convolve_kernel, True), (shape_of((seq_count, channels + PAD, FAST), BF), spec_type), [held, held],
        mixed_grad_rows, filter_spec, first_in, first_out, twist, second_in, second_out,
        flops=1 << 35,
    )
    gated_grad_rows = lax.all_to_all(
        once(gated_grad_rows, query_conv_other), SEQ, split_axis=0, concat_axis=0, tiled=True
    )
    block_output = lax.ppermute(summed, ("zh", "zl"), links(0, 0, True))
    filter_grad = call(
        filter_grad_kernel, shape_of((channels, length), F32), [held],
        mixed_spec, gated_spec, first_out, twist, second_out,
    )
    query_grad, key_grad, value_grad = call(
        last_kernel, (tokens_bf, tokens_bf, tokens_bf), [], key, value, halo, beyond, short_filter,
        once(gated_grad_rows, filter_grad), query_conv_own, query_conv_other, edge_own,
    )
    return (block_output, query_grad, key_grad, value_grad, filter_grad)


def solution(mesh):
    fine = Mesh(mesh.devices.reshape(2, 4, 4, 4, 2), SEQ + CHAN)
    return jax.shard_map(
        shards,
        mesh=fine,
        in_specs=(
            P(SEQ, CHAN),
            P(SEQ, CHAN),
            P(SEQ, CHAN),
            P(None, None, CHAN),
            P(CHAN + SEQ, None),
            P(CHAN, SEQ),
            P(SEQ, CHAN),
        ),
        out_specs=(
            P(SEQ, CHAN),
            P(SEQ, CHAN),
            P(SEQ, CHAN),
            P(SEQ, CHAN),
            P(CHAN + SEQ, None),
        ),
        check_vma=False,
    )
```
